32 devices in a mesh: aux: 32 (over z, y, x, core), occ: 1.
Axes of the slice: x: 2, y: 2, z: 4, core: 2. Of those that a mesh axis runs over, the one named last changes fastest.
Arguments:
- ints: bfloat16 [32, 16, 16, 16384], P(None, None, None, 'aux'), may hold values from -0.125 to 0.125
- blk_atoms: int32 [1024, 2], P('aux'), may hold values from 0 to 255
- blk_count: int32 [32], P('aux'), may hold values from 1 to 32, as said below
- occ_coeff: bfloat16 [1280, 4096], P(None, 'occ'), may hold values from -1.5 to 1.5
- vir_coeff: bfloat16 [4096, 384], P(None, 'occ'), may hold values from -1.5 to 1.5
- batch_ids: int32 [8], replicated, may hold values from 0 to 1279, as said below
Outputs:
- pair_ints: float32 [8, 32, 12, 8, 12], P(None, 'aux', 'occ')
The draws below stay inside these ranges and needn't reach their ends.
Inputs may be any that keep to these rules, and one draw needn't show every extreme that they name: `batch_ids`: the batch's orbitals are distinct, and the batch holds the last occupied orbital. `blk_count`: every owner has at least one live slot, and some owner has all 32 live. Slots of owner g name atoms within 2 * 256 // 32 (at least 2) atoms after atom g * 8, cyclically.
All inputs are finite; a program needn't handle non-finite values.
Results may differ from the reference program's by a relative error of at most 0.0017.
Values may be sent and summed in bfloat16 or wider, within the bound.
No kernel may reach another device: no remote copies, remote signals or barrier semaphores. Data moves between devices by JAX's collectives and lax.ppermute only.
A program may use at most 128 MiB of HBM per device.

```python
import jax
import jax.numpy as jnp
from jax import lax

BS = 16
NATOM = 256
NOCC = 1280
OB = 8
NBLK = 32
AUX_DEV = 512
AV = 12
NGROUP = 32
NAUX = 16384
GROUP = 12
NV = 384
NAO = 4096
N_OCC = 1


def draw_blk_atoms(key, part):
    row_total = NGROUP * NBLK
    owner_ids = jnp.arange(row_total, dtype=jnp.int32) // NBLK
    centre_atom = owner_ids * NATOM // NGROUP
    reach_atoms = max(2 * NATOM // NGROUP, 2)
    offsets = jax.random.randint(key, (row_total, 2), 0, reach_atoms, dtype=jnp.int32)
    return ((centre_atom[:, None] + offsets) % NATOM).astype(jnp.int32)


def draw_blk_count(key, part):
    drawn = jax.random.randint(key, (NGROUP,), 1, NBLK + 1, dtype=jnp.int32)
    squared = jnp.maximum(drawn * drawn // NBLK, 1)
    busiest = jax.random.randint(jax.random.fold_in(key, 7), (), 0, NGROUP, dtype=jnp.int32)
    return jnp.where(jnp.arange(NGROUP, dtype=jnp.int32) == busiest, NBLK, squared).astype(jnp.int32)


def draw_batch_ids(key, part):
    inner_ids = jax.random.permutation(key, NOCC - 1)[:OB - 1].astype(jnp.int32)
    end_ids = jnp.array([NOCC - 1], dtype=jnp.int32)
    joined = jnp.concatenate([end_ids, inner_ids])
    shuffle = jax.random.permutation(jax.random.fold_in(key, 3), OB)
    return joined[shuffle].astype(jnp.int32)


def shard_levels(own_key, extent, shards, smallest, top_value):
    def one(dim, shards_of):
        steps = jax.random.uniform(jax.random.fold_in(jax.random.fold_in(own_key, 6), dim), (shards_of,), jnp.float32, smallest / len(shards), top_value / len(shards))
        return jnp.repeat(jnp.exp(steps), extent[dim] // shards_of).reshape((-1,) + (1,) * (len(extent) - dim - 1))

    level = one(*shards[0])
    for cut in shards[1:]:
        level = level * one(*cut)
    return level


def gaussian(own_key, shape, deviation, bound, cuts=(), kind=jnp.bfloat16):
    values = jax.random.normal(own_key, shape, jnp.float32) * deviation
    if len(cuts) > 0:
        values = shard_levels(own_key, shape, cuts, -0.22, 0.18) * values
    return jnp.clip(values, min=-bound, max=bound).astype(kind)


def setup_inputs(seed: int = 0) -> dict:
    arg_keys = jax.random.split(jax.random.key(seed), 7)
    return {
        "ints": gaussian(arg_keys[0], (NBLK, BS, BS, NAUX), (1.5 * (NBLK * NAUX ** 0.5) ** -0.5), 0.125, ((3, 32),)),
        "blk_atoms": draw_blk_atoms(jax.random.fold_in(arg_keys[6], 71), 0),
        "blk_count": draw_blk_count(jax.random.fold_in(arg_keys[6], 71), 0),
        "occ_coeff": gaussian(arg_keys[3], (NOCC, NAO), BS ** -0.5, 1.5),
        "vir_coeff": gaussian(arg_keys[4], (NAO, NV), BS ** -0.5, 1.5),
        "batch_ids": draw_batch_ids(jax.random.fold_in(arg_keys[6], 71), 0),
    }


def reference(ints, blk_atoms, blk_count, occ_coeff, vir_coeff, batch_ids):
    batch_coeff = occ_coeff[batch_ids]
    per_atom = batch_coeff.reshape(OB, NATOM, BS).astype(jnp.float32)
    vir_atoms = vir_coeff.reshape(NATOM, BS, NV).astype(jnp.float32)

    def owner_fitted(owner_index):
        slot_atoms = lax.dynamic_slice_in_dim(blk_atoms, owner_index * NBLK, NBLK, 0)
        owner_ints = lax.dynamic_slice_in_dim(ints, owner_index * AUX_DEV, AUX_DEV, 3).astype(jnp.float32)
        left_rows = per_atom[:, slot_atoms[:, 0], :]
        half_ints = jnp.einsum('ikm,kmnq->kinq', left_rows, owner_ints)
        live_slots = jnp.arange(NBLK, dtype=jnp.int32) < blk_count[owner_index]
        half_ints = jnp.where(live_slots[:, None, None, None], half_ints, 0.0).astype(jnp.bfloat16)
        half_ints = lax.optimization_barrier(half_ints).astype(jnp.float32)
        right_rows = vir_atoms[slot_atoms[:, 1]]
        return jnp.einsum('knv,kinq->ivq', right_rows, half_ints).astype(jnp.bfloat16)

    fitted = lax.map(owner_fitted, jnp.arange(NGROUP, dtype=jnp.int32))
    arranged = fitted.reshape(NGROUP, OB, N_OCC, NGROUP, AV, AUX_DEV)

    def group_pairs(group_index):
        group_rows = lax.dynamic_index_in_dim(arranged, group_index, 3, keepdims=False)
        group_rows = jnp.transpose(group_rows, (1, 2, 3, 0, 4)).reshape(OB, GROUP, NAUX).astype(jnp.float32)
        return jnp.einsum('icq,jdq->icjd', group_rows, group_rows)

    pair_ints = lax.map(group_pairs, jnp.arange(NGROUP, dtype=jnp.int32))
    return jnp.transpose(pair_ints, (1, 0, 2, 3, 4))
```

```python
import functools

import jax
import jax.numpy as jnp
from jax import lax
from jax.experimental import pallas as pl
from jax.experimental.pallas import tpu as pltpu
from jax.sharding import PartitionSpec as P

LANES = 128
ROWS = 16
WINDOW = 3


def partial_kernel(
    group_width,
    atoms_ref,
    count_ref,
    ids_ref,
    ints_hbm,
    occ_hbm,
    vir_hbm,
    out_ref,
    ints_buf,
    occ_buf,
    vir_buf,
    left_rows,
    left_big,
    right_rows,
    right_t,
    half_buf,
    fit_buf,
    ints_sem,
    occ_sem,
    vir_sem,
):
    slots, depth, aux_local = ints_buf.shape
    batch = occ_buf.shape[0]
    groups = fit_buf.shape[0]
    virs = vir_buf.shape[1]
    owners = lax.axis_size("aux")
    me = lax.axis_index("aux")
    atom_total = occ_hbm.shape[1] // ROWS
    span = occ_hbm.shape[1] // owners
    span_atoms = span // ROWS
    window_atoms = WINDOW * span_atoms

    copies = []
    for i in range(batch):
        base = pl.multiple_of((ids_ref[i] // ROWS) * ROWS, ROWS)
        for b in range(WINDOW):
            start = pl.multiple_of(lax.rem(me + b, owners) * span, LANES)
            copies.append(
                pltpu.make_async_copy(
                    occ_hbm.at[pl.ds(base, ROWS), pl.ds(start, span)],
                    occ_buf.at[i, :, pl.ds(b * span, span)],
                    occ_sem.at[i, b],
                )
            )
    for b in range(WINDOW):
        start = pl.multiple_of(lax.rem(me + b, owners) * span, LANES)
        copies.append(
            pltpu.make_async_copy(
                vir_hbm.at[pl.ds(start, span), :], vir_buf.at[pl.ds(b * span, span), :], vir_sem.at[b]
            )
        )
    for copy in copies:
        copy.start()
    ints_copies = [
        pltpu.make_async_copy(ints_hbm.at[k], ints_buf.at[k], ints_sem.at[k]) for k in range(slots)
    ]
    for copy in ints_copies:
        copy.start()

    def near(slot, side):
        offset = atoms_ref[side, slot] - me * span_atoms
        offset = jnp.where(offset < 0, offset + atom_total, offset)
        return jnp.minimum(offset, window_atoms - 1)

    wide = (groups * ROWS, virs)
    row = lax.broadcasted_iota(jnp.int32, wide, 0)
    col = lax.broadcasted_iota(jnp.int32, wide, 1)
    keep = (row % ROWS < group_width) & (col == (row // ROWS) * group_width + row % ROWS)
    spread = jnp.where(keep, 1.0, 0.0).astype(jnp.bfloat16)

    tall = (window_atoms * batch, batch * ROWS)
    row = lax.broadcasted_iota(jnp.int32, tall, 0) % batch
    col = lax.broadcasted_iota(jnp.int32, tall, 1)
    wanted = jnp.zeros(tall, jnp.int32)
    for i in range(batch):
        wanted = jnp.where(row == i, i * ROWS + ids_ref[i] % ROWS, wanted)
    pick = jnp.where(col == wanted, 1.0, 0.0).astype(jnp.bfloat16)

    shape = (window_atoms * ROWS, depth)
    row = lax.broadcasted_iota(jnp.int32, shape, 0) % ROWS
    col = lax.broadcasted_iota(jnp.int32, shape, 1) // ROWS
    repeat = jnp.where(row == col, 1.0, 0.0).astype(jnp.bfloat16)

    for copy in copies[: batch * WINDOW]:
        copy.wait()
    picked = jnp.dot(
        pick, occ_buf[...].reshape(batch * ROWS, WINDOW * span), preferred_element_type=jnp.float32
    )
    row = lax.broadcasted_iota(jnp.int32, picked.shape, 0) // batch
    col = lax.broadcasted_iota(jnp.int32, picked.shape, 1) // ROWS
    picked = jnp.where(row == col, picked, 0.0).astype(jnp.bfloat16)
    left_rows[...] = jnp.dot(picked, repeat, preferred_element_type=jnp.float32)

    shape = (ROWS, depth)
    diagonal = lax.broadcasted_iota(jnp.int32, shape, 0) == (
        lax.broadcasted_iota(jnp.int32, shape, 1) % ROWS
    )
    for a in range(window_atoms):
        rows = left_rows[a * batch : (a + 1) * batch, :]
        for i in range(batch):
            left_big[a, i * ROWS : (i + 1) * ROWS, :] = jnp.where(
                diagonal, rows[i : i + 1, :], 0.0
            ).astype(jnp.bfloat16)

    for copy in copies[batch * WINDOW :]:
        copy.wait()
    for k in range(slots):
        rows = vir_buf[pl.ds(pl.multiple_of(near(k, 1) * ROWS, ROWS), ROWS), :]
        live = jnp.where(k < count_ref[0], 1.0, 0.0).astype(jnp.bfloat16)
        right_rows[k * ROWS : (k + 1) * ROWS, :] = rows * live
    right_t[...] = lax.dot_general(
        spread, right_rows[...], (((1,), (1,)), ((), ())), preferred_element_type=jnp.float32
    ).astype(jnp.bfloat16)

    for k in range(slots):
        ints_copies[k].wait()
        half = jnp.dot(left_big[near(k, 0)], ints_buf[k], preferred_element_type=jnp.float32)
        half = half.astype(jnp.bfloat16)
        for i in range(batch):
            half_buf[i, k * ROWS : (k + 1) * ROWS, :] = half[i * ROWS : (i + 1) * ROWS, :]

    tile = 256
    for i in range(batch):
        for q in range(0, aux_local, tile):
            fitted = jnp.dot(
                right_t[...], half_buf[i, :, q : q + tile], preferred_element_type=jnp.float32
            ).astype(jnp.bfloat16)
            fit_buf[:, i * ROWS : (i + 1) * ROWS, q : q + tile] = fitted.reshape(groups, ROWS, tile)

    upper = batch // 2 * ROWS
    shape = (upper, LANES)
    row = lax.broadcasted_iota(jnp.int32, shape, 0)
    col = lax.broadcasted_iota(jnp.int32, shape, 1)
    from_below = (col < upper) & (col > row)
    top_half = lax.broadcasted_iota(jnp.int32, (8, LANES), 0) < 4
    for g in range(groups):
        gram = lax.dot_general(
            fit_buf[g], fit_buf[g], (((1,), (1,)), ((), ())), preferred_element_type=jnp.float32
        )
        below = pltpu.roll(gram[upper:, :], upper + 1, 1)
        packed = jnp.where(from_below, below, gram[:upper, :])
        pieces = []
        for i in range(0, batch // 2, 2):
            first = packed[i * ROWS : (i + 1) * ROWS, :]
            second = packed[(i + 1) * ROWS : (i + 2) * ROWS, :]
            mixed = jnp.where(top_half, first[8:, :], pltpu.roll(second[8:, :], 4, 0))
            pieces += [first[:8, :], mixed, second[:8, :]]
        out_ref[g] = jnp.concatenate(pieces, axis=0).astype(jnp.bfloat16)


def partial_sums(ints, blk_atoms, blk_count, occ_coeff, vir_coeff, batch_ids, groups):
    slots, block, _, aux_local = ints.shape
    batch = batch_ids.shape[0]
    virs = vir_coeff.shape[1]
    basis = occ_coeff.shape[1]
    span = basis // groups
    window_atoms = WINDOW * span // block
    depth = block * block
    group_width = virs // groups
    smem = pl.BlockSpec(memory_space=pltpu.SMEM)
    anywhere = pl.BlockSpec(memory_space=pltpu.HBM)
    kept_rows = batch // 2 * group_width
    return pl.pallas_call(
        functools.partial(partial_kernel, group_width),
        out_shape=jax.ShapeDtypeStruct((groups, kept_rows, LANES), jnp.bfloat16),
        in_specs=[smem, smem, smem, anywhere, anywhere, anywhere],
        out_specs=pl.BlockSpec(memory_space=pltpu.VMEM),
        scratch_shapes=[
            pltpu.VMEM((slots, depth, aux_local), jnp.bfloat16),
            pltpu.VMEM((batch, ROWS, WINDOW * span), jnp.bfloat16),
            pltpu.VMEM((WINDOW * span, virs), jnp.bfloat16),
            pltpu.VMEM((window_atoms * batch, depth), jnp.float32),
            pltpu.VMEM((window_atoms, batch * ROWS, depth), jnp.bfloat16),
            pltpu.VMEM((slots * ROWS, virs), jnp.bfloat16),
            pltpu.VMEM((groups * ROWS, slots * ROWS), jnp.bfloat16),
            pltpu.VMEM((batch, slots * ROWS, aux_local), jnp.bfloat16),
            pltpu.VMEM((groups, batch * ROWS, aux_local), jnp.bfloat16),
            pltpu.SemaphoreType.DMA((slots,)),
            pltpu.SemaphoreType.DMA((batch, WINDOW)),
            pltpu.SemaphoreType.DMA((WINDOW,)),
        ],
        compiler_params=pltpu.CompilerParams(vmem_limit_bytes=40 * 1024 * 1024),
    )(
        blk_atoms.T,
        blk_count,
        batch_ids,
        ints.reshape(slots, depth, aux_local),
        occ_coeff,
        vir_coeff,
    )


def total_kernel(group_width, batch, parts_ref, out_ref):
    total = jnp.sum(parts_ref[...].astype(jnp.float32), axis=0)
    upper = batch // 2 * ROWS
    top_half = lax.broadcasted_iota(jnp.int32, (8, LANES), 0) < 4
    pieces = []
    for i in range(0, batch // 2, 2):
        first, mixed, second = (
            total[(3 * (i // 2) + s) * 8 : (3 * (i // 2) + s + 1) * 8, :] for s in range(3)
        )
        pieces += [
            first,
            jnp.where(top_half, mixed, 0.0),
            second,
            jnp.where(top_half, pltpu.roll(mixed, 4, 0), 0.0),
        ]
    above = jnp.concatenate(pieces, axis=0)
    both = jnp.concatenate([above, pltpu.roll(above, upper - 1, 1)], axis=0)
    shape = (2 * upper, 2 * upper)
    row = lax.broadcasted_iota(jnp.int32, shape, 0)
    col = lax.broadcasted_iota(jnp.int32, shape, 1)
    direct = ((row < upper) & ((col >= upper) | (col <= row))) | ((row >= upper) & (col >= row))
    whole = jnp.where(direct, both, both.T)
    for i in range(batch):
        for c in range(0, group_width, 8):
            rows = whole[i * ROWS + c : i * ROWS + c + 8, :]
            count = min(8, group_width - c)
            for j in range(batch):
                moved = rows if j == 0 else pltpu.roll(rows, LANES - j * ROWS, 1)
                start = (i * group_width + c) * batch + j
                out_ref[pl.ds(start, count, stride=batch), :] = moved[:count, :group_width]


def total_sums(parts, batch, group_width):
    return pl.pallas_call(
        functools.partial(total_kernel, group_width, batch),
        out_shape=jax.ShapeDtypeStruct((batch * group_width * batch, group_width), jnp.float32),
        in_specs=[pl.BlockSpec(memory_space=pltpu.VMEM)],
        out_specs=pl.BlockSpec(memory_space=pltpu.VMEM),
    )(parts)


def half_transform(left_rows, right_rows, block_ints, live_count):
    half_ints = jnp.einsum(
        "ikm,kmnq->kinq", left_rows, block_ints, preferred_element_type=jnp.float32
    )
    slot_ids = jnp.arange(block_ints.shape[0], dtype=jnp.int32)
    half_ints = jnp.where((slot_ids < live_count)[:, None, None, None], half_ints, 0.0).astype(
        jnp.bfloat16
    )
    return jnp.einsum("knv,kinq->ivq", right_rows, half_ints, preferred_element_type=jnp.float32)


def regrouping_device(ints, blk_atoms, blk_count, occ_coeff, vir_coeff, batch_ids):
    batch_size = batch_ids.shape[0]
    block_size = ints.shape[1]
    aux_local = ints.shape[3]
    picked = jnp.take(occ_coeff, batch_ids, axis=0)
    batch_coeff = lax.all_gather(picked, "occ", axis=1, tiled=True)
    atom_total = batch_coeff.shape[1] // block_size
    left_all = batch_coeff.reshape(batch_size, atom_total, block_size)[:, blk_atoms[:, 0], :]
    vir_local = vir_coeff.shape[1]
    right_all = vir_coeff.reshape(atom_total, block_size, vir_local)[blk_atoms[:, 1]]
    live_count = blk_count[0]
    summed = half_transform(left_all, right_all, ints, live_count)
    group_count = lax.axis_size("aux")
    vir_group = vir_local // group_count
    fitted = summed.astype(jnp.bfloat16).reshape(batch_size, group_count, vir_group, aux_local)
    regrouped = lax.all_to_all(
        lax.all_to_all(fitted, "aux", split_axis=1, concat_axis=3, tiled=True),
        "occ",
        split_axis=3,
        concat_axis=2,
        tiled=True,
    )
    group_rows = regrouped[:, 0]
    group_width = group_rows.shape[1]
    flat_rows = group_rows.reshape(batch_size * group_width, group_rows.shape[2])
    kept_rows = lax.psum_scatter(
        jnp.einsum("icq,xq->cix", group_rows, flat_rows, preferred_element_type=jnp.float32),
        "occ",
        scatter_dimension=0,
        tiled=True,
    )
    pair_ints = jnp.transpose(
        kept_rows.reshape(vir_group, batch_size, batch_size, group_width), (1, 0, 2, 3)
    )[:, None]
    return pair_ints


def on_device(ints, blk_atoms, blk_count, occ_coeff, vir_coeff, batch_ids):
    if lax.axis_size("occ") > 1:
        return regrouping_device(ints, blk_atoms, blk_count, occ_coeff, vir_coeff, batch_ids)
    batch = batch_ids.shape[0]
    groups = lax.axis_size("aux")
    group_width = vir_coeff.shape[1] // groups
    parts = partial_sums(ints, blk_atoms, blk_count, occ_coeff, vir_coeff, batch_ids, groups)
    parts = lax.all_to_all(parts, "aux", split_axis=0, concat_axis=0, tiled=True)
    total = total_sums(parts, batch, group_width)
    return total.reshape(batch, 1, group_width, batch, group_width)


def solution(mesh):
    in_specs = (
        P(None, None, None, "aux"),
        P("aux", None),
        P("aux"),
        P(None, "occ"),
        P(None, "occ"),
        P(),
    )
    out_specs = P(None, "aux", "occ", None, None)
    return jax.shard_map(
        on_device, mesh=mesh, in_specs=in_specs, out_specs=out_specs, check_vma=False
    )
```

```python
import functools

import jax
import jax.numpy as jnp
from jax import lax
from jax.experimental import pallas as pl
from jax.experimental.pallas import tpu as pltpu
from jax.sharding import PartitionSpec as P

LANES = 128
ROWS = 16
WINDOW = 3
CHUNKS = 1
PARTS = 2
EARLY = 1
PRIO = 1
TILE = 256


def partial_kernel(
    group_width,
    atoms_hbm,
    count_hbm,
    ids_hbm,
    ints_hbm,
    occ_hbm,
    vir_hbm,
    keep_ref,
    send_ref,
    atoms_ref,
    count_ref,
    ids_ref,
    ints_buf,
    occ_buf,
    vir_buf,
    left_rows,
    left_big,
    right_rows,
    right_t,
    half_buf,
    fit_buf,
    small_sem,
    ints_sem,
    occ_sem,
    vir_sem,
):
    slots, depth, aux_local = ints_buf.shape
    batch = occ_buf.shape[0]
    groups = fit_buf.shape[0]
    virs = vir_buf.shape[1]
    owners = lax.axis_size("aux")
    me = lax.axis_index("aux")
    atom_total = occ_hbm.shape[1] // ROWS
    span = occ_hbm.shape[1] // owners
    span_atoms = span // ROWS
    window_atoms = left_big.shape[0]
    step = slots // CHUNKS
    part = aux_local // PARTS

    small_copies = [
        pltpu.make_async_copy(source, target, small_sem.at[s])
        for s, (source, target) in enumerate(
            ((ids_hbm, ids_ref), (atoms_hbm, atoms_ref), (count_hbm, count_ref))
        )
    ]
    for copy in small_copies:
        copy.start()
    starts = [pl.multiple_of(lax.rem(me + b, owners) * span, LANES) for b in range(WINDOW)]
    vir_copies = [
        pltpu.make_async_copy(
            vir_hbm.at[pl.ds(starts[b], span), :], vir_buf.at[pl.ds(b * span, span), :], vir_sem.at[b]
        )
        for b in range(WINDOW)
    ]
    for copy in vir_copies:
        copy.start()
    ints_copies = []
    for p in range(PARTS):
        for c in range(CHUNKS):
            block = (pl.ds(c * step, step), slice(None), pl.ds(p * part, part))
            ints_copies.append(
                pltpu.make_async_copy(ints_hbm.at[block], ints_buf.at[block], ints_sem.at[p, c])
            )
    for copy in ints_copies[:EARLY]:
        copy.start(priority=PRIO)
    small_copies[0].wait()
    occ_copies = []
    for i in range(batch):
        base = pl.multiple_of(ids_ref[i] & -ROWS, ROWS)
        for b in range(WINDOW):
            occ_copies.append(
                pltpu.make_async_copy(
                    occ_hbm.at[pl.ds(base, ROWS), pl.ds(starts[b], span)],
                    occ_buf.at[i, :, pl.ds(b * span, span)],
                    occ_sem.at[i, b],
                )
            )
    for copy in occ_copies:
        copy.start()
    for copy in ints_copies[EARLY:]:
        copy.start(priority=PRIO)
    for copy in small_copies[1:]:
        copy.wait()

    def near(slot, side):
        offset = atoms_ref[side, slot] - me * span_atoms
        offset = jnp.where(offset < 0, offset + atom_total, offset)
        return jnp.minimum(offset, window_atoms - 1)

    row_bits = ROWS.bit_length() - 1
    batch_bits = batch.bit_length() - 1
    wide = (groups * ROWS, virs)
    row = lax.broadcasted_iota(jnp.int32, wide, 0)
    col = lax.broadcasted_iota(jnp.int32, wide, 1)
    inner = row & (ROWS - 1)
    target = jnp.where(inner < group_width, (row >> row_bits) * group_width + inner, -1)
    spread = jnp.where(col == target, 1.0, 0.0).astype(jnp.bfloat16)

    shape = (WINDOW * span, depth)
    row = lax.broadcasted_iota(jnp.int32, shape, 0) & (ROWS - 1)
    col = lax.broadcasted_iota(jnp.int32, shape, 1) >> row_bits
    repeat = jnp.where(row == col, 1.0, 0.0).astype(jnp.bfloat16)

    tall = (batch, batch * ROWS)
    row = lax.broadcasted_iota(jnp.int32, tall, 0)
    col = lax.broadcasted_iota(jnp.int32, tall, 1)
    wanted = jnp.zeros(tall, jnp.int32)
    for i in range(batch):
        wanted = jnp.where(row == i, i * ROWS + (ids_ref[i] & (ROWS - 1)), wanted)
    pick = jnp.where(col == wanted, 1.0, 0.0).astype(jnp.bfloat16)

    for copy in vir_copies:
        copy.wait()
    for k in range(slots):
        rows = vir_buf[pl.ds(pl.multiple_of(near(k, 1) * ROWS, ROWS), ROWS), :]
        live = jnp.where(k < count_ref[0], 1.0, 0.0).astype(jnp.bfloat16)
        right_rows[k * ROWS : (k + 1) * ROWS, :] = rows * live
    right_t[...] = lax.dot_general(
        spread, right_rows[...], (((1,), (1,)), ((), ())), preferred_element_type=jnp.float32
    ).astype(jnp.bfloat16)

    for copy in occ_copies:
        copy.wait()
    picked = jnp.dot(
        pick, occ_buf[...].reshape(batch * ROWS, WINDOW * span), preferred_element_type=jnp.float32
    )
    picked = jnp.concatenate([picked] * window_atoms, axis=0)
    row = lax.broadcasted_iota(jnp.int32, picked.shape, 0) >> batch_bits
    col = lax.broadcasted_iota(jnp.int32, picked.shape, 1) >> row_bits
    picked = jnp.where(row == col, picked, 0.0).astype(jnp.bfloat16)
    left_rows[...] = jnp.dot(picked, repeat, preferred_element_type=jnp.float32)

    shape = (ROWS, depth)
    diagonal = lax.broadcasted_iota(jnp.int32, shape, 0) == (
        lax.broadcasted_iota(jnp.int32, shape, 1) & (ROWS - 1)
    )
    for a in range(window_atoms):
        rows = left_rows[a * batch : (a + 1) * batch, :]
        for i in range(batch):
            left_big[a, i * ROWS : (i + 1) * ROWS, :] = jnp.where(
                diagonal, rows[i : i + 1, :], 0.0
            ).astype(jnp.bfloat16)

    for p in range(PARTS):
        cols = slice(p * part, (p + 1) * part)
        for c in range(CHUNKS):
            ints_copies[p * CHUNKS + c].wait()
            for k in range(c * step, (c + 1) * step):
                half = jnp.dot(
                    left_big[near(k, 0)], ints_buf[k, :, cols], preferred_element_type=jnp.float32
                ).astype(jnp.bfloat16)
                for i in range(batch):
                    half_buf[i, k * ROWS : (k + 1) * ROWS, cols] = half[i * ROWS : (i + 1) * ROWS, :]
        for i in range(batch):
            for q in range(p * part, (p + 1) * part, TILE):
                fitted = jnp.dot(
                    right_t[...], half_buf[i, :, q : q + TILE], preferred_element_type=jnp.float32
                ).astype(jnp.bfloat16)
                fit_buf[:, i * ROWS : (i + 1) * ROWS, q : q + TILE] = fitted.reshape(
                    groups, ROWS, TILE
                )

    upper = batch // 2 * ROWS
    shape = (upper, LANES)
    row = lax.broadcasted_iota(jnp.int32, shape, 0)
    col = lax.broadcasted_iota(jnp.int32, shape, 1)
    from_below = (col < upper) & (col > row)
    top_half = lax.broadcasted_iota(jnp.int32, (8, LANES), 0) < 4
    own = lax.rem(me, 2)
    high = batch * ROWS
    for first_group in range(0, groups, 2):
        both = fit_buf[first_group : first_group + 2].reshape(2 * high, aux_local)
        grams = lax.dot_general(
            both, both, (((1,), (1,)), ((), ())), preferred_element_type=jnp.float32
        )
        for g in range(2):
            gram = grams[g * high : (g + 1) * high, g * high : (g + 1) * high]
            below = pltpu.roll(gram[upper:, :], upper + 1, 1)
            packed = jnp.where(from_below, below, gram[:upper, :])
            halves = []
            for i in range(0, batch // 2, 2):
                first = packed[i * ROWS : (i + 1) * ROWS, :]
                second = packed[(i + 1) * ROWS : (i + 2) * ROWS, :]
                mixed = jnp.where(top_half, first[8:, :], pltpu.roll(second[8:, :], 4, 0))
                halves.append(jnp.concatenate([first[:8, :], mixed, second[:8, :]], axis=0))
            keep_ref[first_group + g] = jnp.where(own == 0, halves[0], halves[1])
            send_ref[first_group + g] = jnp.where(own == 0, halves[1], halves[0])


def partial_sums(ints, blk_atoms, blk_count, occ_coeff, vir_coeff, batch_ids, groups):
    slots, block, _, aux_local = ints.shape
    batch = batch_ids.shape[0]
    virs = vir_coeff.shape[1]
    basis = occ_coeff.shape[1]
    span = basis // groups
    window_atoms = (WINDOW - 1) * span // block + 1
    depth = block * block
    group_width = virs // groups
    far = pl.BlockSpec(memory_space=pltpu.HBM)
    result = jax.ShapeDtypeStruct((groups, batch // 4 * group_width, LANES), jnp.float32)
    return pl.pallas_call(
        functools.partial(partial_kernel, group_width),
        out_shape=(result, result),
        in_specs=[far] * 6,
        out_specs=[pl.BlockSpec(memory_space=pltpu.VMEM)] * 2,
        scratch_shapes=[
            pltpu.SMEM((2, slots), jnp.int32),
            pltpu.SMEM((1,), jnp.int32),
            pltpu.SMEM((batch,), jnp.int32),
            pltpu.VMEM((slots, depth, aux_local), jnp.bfloat16),
            pltpu.VMEM((batch, ROWS, WINDOW * span), jnp.bfloat16),
            pltpu.VMEM((WINDOW * span, virs), jnp.bfloat16),
            pltpu.VMEM((window_atoms * batch, depth), jnp.float32),
            pltpu.VMEM((window_atoms, batch * ROWS, depth), jnp.bfloat16),
            pltpu.VMEM((slots * ROWS, virs), jnp.bfloat16),
            pltpu.VMEM((groups * ROWS, slots * ROWS), jnp.bfloat16),
            pltpu.VMEM((batch, slots * ROWS, aux_local), jnp.bfloat16),
            pltpu.VMEM((groups, batch * ROWS, aux_local), jnp.bfloat16),
            pltpu.SemaphoreType.DMA((3,)),
            pltpu.SemaphoreType.DMA((PARTS, CHUNKS)),
            pltpu.SemaphoreType.DMA((batch, WINDOW)),
            pltpu.SemaphoreType.DMA((WINDOW,)),
        ],
        compiler_params=pltpu.CompilerParams(vmem_limit_bytes=63 * 1024 * 1024),
    )(
        blk_atoms.T,
        blk_count,
        batch_ids,
        ints.reshape(slots, depth, aux_local),
        occ_coeff,
        vir_coeff,
    )


def total_kernel(group_width, batch, parts_ref, out_ref):
    owners, rows, _ = parts_ref.shape
    total = jnp.sum(
        parts_ref[...].astype(jnp.float32).reshape(owners // 2, 2 * rows, LANES), axis=0
    )
    upper = batch // 2 * ROWS
    top_half = lax.broadcasted_iota(jnp.int32, (8, LANES), 0) < 4
    pieces = []
    for i in range(0, batch // 2, 2):
        first, mixed, second = (
            total[(3 * (i // 2) + s) * 8 : (3 * (i // 2) + s + 1) * 8, :] for s in range(3)
        )
        pieces += [
            first,
            jnp.where(top_half, mixed, 0.0),
            second,
            jnp.where(top_half, pltpu.roll(mixed, 4, 0), 0.0),
        ]
    above = jnp.concatenate(pieces, axis=0)
    both = jnp.concatenate([above, pltpu.roll(above, upper - 1, 1)], axis=0)
    shape = (2 * upper, 2 * upper)
    row = lax.broadcasted_iota(jnp.int32, shape, 0)
    col = lax.broadcasted_iota(jnp.int32, shape, 1)
    direct = ((row < upper) & ((col >= upper) | (col <= row))) | ((row >= upper) & (col >= row))
    whole = jnp.where(direct, both, both.T)
    for i in range(batch):
        for c in range(0, group_width, 8):
            rows = whole[i * ROWS + c : i * ROWS + c + 8, :]
            count = min(8, group_width - c)
            for j in range(batch):
                moved = rows if j == 0 else pltpu.roll(rows, LANES - j * ROWS, 1)
                start = (i * group_width + c) * batch + j
                out_ref[pl.ds(start, count, stride=batch), :] = moved[:count, :group_width]


def total_sums(parts, batch, group_width):
    return pl.pallas_call(
        functools.partial(total_kernel, group_width, batch),
        out_shape=jax.ShapeDtypeStruct((batch * group_width * batch, group_width), jnp.float32),
        in_specs=[pl.BlockSpec(memory_space=pltpu.VMEM)],
        out_specs=pl.BlockSpec(memory_space=pltpu.VMEM),
    )(parts)


def half_transform(left_rows, right_rows, block_ints, live_count):
    half_ints = jnp.einsum(
        "ikm,kmnq->kinq", left_rows, block_ints, preferred_element_type=jnp.float32
    )
    slot_ids = jnp.arange(block_ints.shape[0], dtype=jnp.int32)
    half_ints = jnp.where((slot_ids < live_count)[:, None, None, None], half_ints, 0.0).astype(
        jnp.bfloat16
    )
    return jnp.einsum("knv,kinq->ivq", right_rows, half_ints, preferred_element_type=jnp.float32)


def regrouping_device(ints, blk_atoms, blk_count, occ_coeff, vir_coeff, batch_ids):
    batch_size = batch_ids.shape[0]
    block_size = ints.shape[1]
    aux_local = ints.shape[3]
    picked = jnp.take(occ_coeff, batch_ids, axis=0)
    batch_coeff = lax.all_gather(picked, "occ", axis=1, tiled=True)
    atom_total = batch_coeff.shape[1] // block_size
    left_all = batch_coeff.reshape(batch_size, atom_total, block_size)[:, blk_atoms[:, 0], :]
    vir_local = vir_coeff.shape[1]
    right_all = vir_coeff.reshape(atom_total, block_size, vir_local)[blk_atoms[:, 1]]
    live_count = blk_count[0]
    summed = half_transform(left_all, right_all, ints, live_count)
    group_count = lax.axis_size("aux")
    vir_group = vir_local // group_count
    fitted = summed.astype(jnp.bfloat16).reshape(batch_size, group_count, vir_group, aux_local)
    regrouped = lax.all_to_all(
        lax.all_to_all(fitted, "aux", split_axis=1, concat_axis=3, tiled=True),
        "occ",
        split_axis=3,
        concat_axis=2,
        tiled=True,
    )
    group_rows = regrouped[:, 0]
    group_width = group_rows.shape[1]
    flat_rows = group_rows.reshape(batch_size * group_width, group_rows.shape[2])
    kept_rows = lax.psum_scatter(
        jnp.einsum("icq,xq->cix", group_rows, flat_rows, preferred_element_type=jnp.float32),
        "occ",
        scatter_dimension=0,
        tiled=True,
    )
    pair_ints = jnp.transpose(
        kept_rows.reshape(vir_group, batch_size, batch_size, group_width), (1, 0, 2, 3)
    )[:, None]
    return pair_ints


def on_device(ints, blk_atoms, blk_count, occ_coeff, vir_coeff, batch_ids):
    if lax.axis_size("occ") > 1:
        return regrouping_device(ints, blk_atoms, blk_count, occ_coeff, vir_coeff, batch_ids)
    batch = batch_ids.shape[0]
    groups = lax.axis_size("aux")
    group_width = vir_coeff.shape[1] // groups
    keep, send = partial_sums(ints, blk_atoms, blk_count, occ_coeff, vir_coeff, batch_ids, groups)
    partners = [(owner, owner ^ 1) for owner in range(groups)]
    parts = (keep + lax.ppermute(send, "aux", partners)).astype(jnp.bfloat16)
    parts = lax.all_to_all(parts, "aux", split_axis=0, concat_axis=0, tiled=True)
    total = total_sums(parts, batch, group_width)
    return total.reshape(batch, 1, group_width, batch, group_width)


def solution(mesh):
    in_specs = (
        P(None, None, None, "aux"),
        P("aux", None),
        P("aux"),
        P(None, "occ"),
        P(None, "occ"),
        P(),
    )
    out_specs = P(None, "aux", "occ", None, None)
    return jax.shard_map(
        on_device, mesh=mesh, in_specs=in_specs, out_specs=out_specs, check_vma=False
    )
```

```python
import functools

import jax
import jax.numpy as jnp
from jax import lax
from jax.experimental import pallas as pl
from jax.experimental.pallas import tpu as pltpu
from jax.sharding import PartitionSpec as P

LANES = 128
ROWS = 16
WINDOW = 3
CHUNKS = 1
PARTS = 2
EARLY = 1
PRIO = 1
TILE = 256


def partial_kernel(
    group_width,
    atoms_hbm,
    count_hbm,
    ids_hbm,
    ints_hbm,
    occ_hbm,
    vir_hbm,
    keep_ref,
    send_ref,
    atoms_ref,
    count_ref,
    ids_ref,
    ints_buf,
    occ_buf,
    vir_buf,
    left_rows,
    left_big,
    right_rows,
    right_t,
    half_buf,
    fit_buf,
    small_sem,
    ints_sem,
    occ_sem,
    vir_sem,
):
    slots, depth, aux_local = ints_buf.shape
    batch = occ_buf.shape[0]
    groups = fit_buf.shape[0]
    virs = vir_buf.shape[1]
    owners = lax.axis_size("aux")
    me = lax.axis_index("aux")
    atom_total = occ_hbm.shape[1] // ROWS
    span = occ_hbm.shape[1] // owners
    span_atoms = span // ROWS
    window_atoms = left_big.shape[0]
    step = slots // CHUNKS
    part = aux_local // PARTS

    small_copies = [
        pltpu.make_async_copy(source, target, small_sem.at[s])
        for s, (source, target) in enumerate(
            ((ids_hbm, ids_ref), (atoms_hbm, atoms_ref), (count_hbm, count_ref))
        )
    ]
    for copy in small_copies:
        copy.start()
    starts = [pl.multiple_of(lax.rem(me + b, owners) * span, LANES) for b in range(WINDOW)]
    vir_copies = [
        pltpu.make_async_copy(
            vir_hbm.at[pl.ds(starts[b], span), :], vir_buf.at[pl.ds(b * span, span), :], vir_sem.at[b]
        )
        for b in range(WINDOW)
    ]
    for copy in vir_copies:
        copy.start()
    ints_copies = []
    for p in range(PARTS):
        for c in range(CHUNKS):
            block = (pl.ds(c * step, step), slice(None), pl.ds(p * part, part))
            ints_copies.append(
                pltpu.make_async_copy(ints_hbm.at[block], ints_buf.at[block], ints_sem.at[p, c])
            )
    for copy in ints_copies[:EARLY]:
        copy.start(priority=PRIO)
    small_copies[0].wait()
    occ_copies = []
    for i in range(batch):
        base = pl.multiple_of(ids_ref[i] & -ROWS, ROWS)
        for b in range(WINDOW):
            occ_copies.append(
                pltpu.make_async_copy(
                    occ_hbm.at[pl.ds(base, ROWS), pl.ds(starts[b], span)],
                    occ_buf.at[i, :, pl.ds(b * span, span)],
                    occ_sem.at[i, b],
                )
            )
    for copy in occ_copies:
        copy.start()
    for copy in ints_copies[EARLY:]:
        copy.start(priority=PRIO)
    for copy in small_copies[1:]:
        copy.wait()

    def near(slot, side):
        offset = atoms_ref[side, slot] - me * span_atoms
        offset = jnp.where(offset < 0, offset + atom_total, offset)
        return jnp.minimum(offset, window_atoms - 1)

    row_bits = ROWS.bit_length() - 1
    batch_bits = batch.bit_length() - 1
    quad = 4 * group_width
    wide = (quad, virs)
    row = lax.broadcasted_iota(jnp.int32, wide, 0)
    col = lax.broadcasted_iota(jnp.int32, wide, 1)
    low = (row >> 3) * group_width + (row & 7)
    high = ((row - 32) >> 2) * group_width + 8 + (row & 3)
    target = jnp.where(row < 32, low, high) - col
    spread = jnp.concatenate(
        [jnp.where(target == -start, 1.0, 0.0).astype(jnp.bfloat16) for start in range(0, virs, quad)],
        axis=0,
    )

    shape = (WINDOW * span, depth)
    row = lax.broadcasted_iota(jnp.int32, shape, 0) & (ROWS - 1)
    col = lax.broadcasted_iota(jnp.int32, shape, 1) >> row_bits
    repeat = jnp.where(row == col, 1.0, 0.0).astype(jnp.bfloat16)

    tall = (batch, batch * ROWS)
    row = lax.broadcasted_iota(jnp.int32, tall, 0)
    col = lax.broadcasted_iota(jnp.int32, tall, 1)
    wanted = jnp.zeros(tall, jnp.int32)
    for i in range(batch):
        wanted = jnp.where(row == i, i * ROWS + (ids_ref[i] & (ROWS - 1)), wanted)
    pick = jnp.where(col == wanted, 1.0, 0.0).astype(jnp.bfloat16)

    for copy in vir_copies:
        copy.wait()
    for k in range(slots):
        rows = vir_buf[pl.ds(pl.multiple_of(near(k, 1) * ROWS, ROWS), ROWS), :]
        live = jnp.where(k < count_ref[0], 1.0, 0.0).astype(jnp.bfloat16)
        right_rows[k * ROWS : (k + 1) * ROWS, :] = rows * live
    right_t[...] = lax.dot_general(
        spread, right_rows[...], (((1,), (1,)), ((), ())), preferred_element_type=jnp.float32
    ).astype(jnp.bfloat16)

    for copy in occ_copies:
        copy.wait()
    picked = jnp.dot(
        pick, occ_buf[...].reshape(batch * ROWS, WINDOW * span), preferred_element_type=jnp.float32
    )
    picked = jnp.concatenate([picked] * window_atoms, axis=0)
    row = lax.broadcasted_iota(jnp.int32, picked.shape, 0) >> batch_bits
    col = lax.broadcasted_iota(jnp.int32, picked.shape, 1) >> row_bits
    picked = jnp.where(row == col, picked, 0.0).astype(jnp.bfloat16)
    left_rows[...] = jnp.dot(picked, repeat, preferred_element_type=jnp.float32)

    shape = (ROWS, depth)
    diagonal = lax.broadcasted_iota(jnp.int32, shape, 0) == (
        lax.broadcasted_iota(jnp.int32, shape, 1) & (ROWS - 1)
    )
    for a in range(window_atoms):
        rows = left_rows[a * batch : (a + 1) * batch, :]
        for i in range(batch):
            left_big[a, i * ROWS : (i + 1) * ROWS, :] = jnp.where(
                diagonal, rows[i : i + 1, :], 0.0
            ).astype(jnp.bfloat16)

    for p in range(PARTS):
        cols = slice(p * part, (p + 1) * part)
        for c in range(CHUNKS):
            ints_copies[p * CHUNKS + c].wait()
            for k in range(c * step, (c + 1) * step):
                half = jnp.dot(
                    left_big[near(k, 0)], ints_buf[k, :, cols], preferred_element_type=jnp.float32
                ).astype(jnp.bfloat16)
                for i in range(batch):
                    half_buf[i, k * ROWS : (k + 1) * ROWS, cols] = half[i * ROWS : (i + 1) * ROWS, :]
        for i in range(batch):
            for q in range(p * part, (p + 1) * part, TILE):
                fitted = jnp.dot(
                    right_t[...], half_buf[i, :, q : q + TILE], preferred_element_type=jnp.float32
                )
                for g in range(groups):
                    start = g // 4 * quad
                    low = fitted[start + g % 4 * 8 : start + g % 4 * 8 + 8, :]
                    start += 32 + g % 4 // 2 * 8
                    high = fitted[start : start + 8, :]
                    if g % 2 == 1:
                        high = pltpu.roll(high, 4, 0)
                    fit_buf[g, i * ROWS : (i + 1) * ROWS, q : q + TILE] = jnp.concatenate(
                        [low, high], axis=0
                    ).astype(jnp.bfloat16)

    upper = batch // 2 * ROWS
    shape = (upper, LANES)
    row = lax.broadcasted_iota(jnp.int32, shape, 0)
    col = lax.broadcasted_iota(jnp.int32, shape, 1)
    from_below = (col < upper) & (col > row)
    top_half = lax.broadcasted_iota(jnp.int32, (8, LANES), 0) < 4
    own = lax.rem(me, 2)
    high = batch * ROWS
    for first_group in range(0, groups, 2):
        both = fit_buf[first_group : first_group + 2].reshape(2 * high, aux_local)
        grams = lax.dot_general(
            both, both, (((1,), (1,)), ((), ())), preferred_element_type=jnp.float32
        )
        for g in range(2):
            gram = grams[g * high : (g + 1) * high, g * high : (g + 1) * high]
            below = pltpu.roll(gram[upper:, :], upper + 1, 1)
            packed = jnp.where(from_below, below, gram[:upper, :])
            halves = []
            for i in range(0, batch // 2, 2):
                first = packed[i * ROWS : (i + 1) * ROWS, :]
                second = packed[(i + 1) * ROWS : (i + 2) * ROWS, :]
                mixed = jnp.where(top_half, first[8:, :], pltpu.roll(second[8:, :], 4, 0))
                halves.append(jnp.concatenate([first[:8, :], mixed, second[:8, :]], axis=0))
            keep_ref[first_group + g] = jnp.where(own == 0, halves[0], halves[1])
            send_ref[first_group + g] = jnp.where(own == 0, halves[1], halves[0])


def in_place(operand):
    return pltpu.with_memory_space_constraint(operand, pltpu.HBM)


def partial_sums(ints, blk_atoms, blk_count, occ_coeff, vir_coeff, batch_ids, groups):
    slots, block, _, aux_local = ints.shape
    batch = batch_ids.shape[0]
    virs = vir_coeff.shape[1]
    basis = occ_coeff.shape[1]
    span = basis // groups
    window_atoms = (WINDOW - 1) * span // block + 1
    depth = block * block
    group_width = virs // groups
    far = pl.BlockSpec(memory_space=pltpu.HBM)
    result = jax.ShapeDtypeStruct((groups, batch // 4 * group_width, LANES), jnp.float32)
    return pl.pallas_call(
        functools.partial(partial_kernel, group_width),
        out_shape=(result, result),
        in_specs=[far] * 6,
        out_specs=[pl.BlockSpec(memory_space=pltpu.VMEM)] * 2,
        scratch_shapes=[
            pltpu.SMEM((2, slots), jnp.int32),
            pltpu.SMEM((1,), jnp.int32),
            pltpu.SMEM((batch,), jnp.int32),
            pltpu.VMEM((slots, depth, aux_local), jnp.bfloat16),
            pltpu.VMEM((batch, ROWS, WINDOW * span), jnp.bfloat16),
            pltpu.VMEM((WINDOW * span, virs), jnp.bfloat16),
            pltpu.VMEM((window_atoms * batch, depth), jnp.float32),
            pltpu.VMEM((window_atoms, batch * ROWS, depth), jnp.bfloat16),
            pltpu.VMEM((slots * ROWS, virs), jnp.bfloat16),
            pltpu.VMEM((virs, slots * ROWS), jnp.bfloat16),
            pltpu.VMEM((batch, slots * ROWS, aux_local), jnp.bfloat16),
            pltpu.VMEM((groups, batch * ROWS, aux_local), jnp.bfloat16),
            pltpu.SemaphoreType.DMA((3,)),
            pltpu.SemaphoreType.DMA((PARTS, CHUNKS)),
            pltpu.SemaphoreType.DMA((batch, WINDOW)),
            pltpu.SemaphoreType.DMA((WINDOW,)),
        ],
        compiler_params=pltpu.CompilerParams(vmem_limit_bytes=40 * 1024 * 1024),
    )(
        in_place(blk_atoms.T),
        blk_count,
        in_place(batch_ids),
        in_place(ints.reshape(slots, depth, aux_local)),
        in_place(occ_coeff),
        in_place(vir_coeff),
    )


def total_kernel(group_width, batch, parts_ref, out_ref):
    owners, rows, _ = parts_ref.shape
    total = jnp.sum(
        parts_ref[...].astype(jnp.float32).reshape(owners // 2, 2 * rows, LANES), axis=0
    )
    upper = batch // 2 * ROWS
    top_half = lax.broadcasted_iota(jnp.int32, (8, LANES), 0) < 4
    pieces = []
    for i in range(0, batch // 2, 2):
        first, mixed, second = (
            total[(3 * (i // 2) + s) * 8 : (3 * (i // 2) + s + 1) * 8, :] for s in range(3)
        )
        pieces += [
            first,
            jnp.where(top_half, mixed, 0.0),
            second,
            jnp.where(top_half, pltpu.roll(mixed, 4, 0), 0.0),
        ]
    above = jnp.concatenate(pieces, axis=0)
    both = jnp.concatenate([above, pltpu.roll(above, upper - 1, 1)], axis=0)
    shape = (2 * upper, 2 * upper)
    row = lax.broadcasted_iota(jnp.int32, shape, 0)
    col = lax.broadcasted_iota(jnp.int32, shape, 1)
    direct = ((row < upper) & ((col >= upper) | (col <= row))) | ((row >= upper) & (col >= row))
    whole = jnp.where(direct, both, both.T)
    for i in range(batch):
        for c in range(0, group_width, 8):
            rows = whole[i * ROWS + c : i * ROWS + c + 8, :]
            count = min(8, group_width - c)
            for j in range(batch):
                moved = rows if j == 0 else pltpu.roll(rows, LANES - j * ROWS, 1)
                start = (i * group_width + c) * batch + j
                out_ref[pl.ds(start, count, stride=batch), :] = moved[:count, :group_width]


def total_sums(parts, batch, group_width):
    return pl.pallas_call(
        functools.partial(total_kernel, group_width, batch),
        out_shape=jax.ShapeDtypeStruct((batch * group_width * batch, group_width), jnp.float32),
        in_specs=[pl.BlockSpec(memory_space=pltpu.VMEM)],
        out_specs=pl.BlockSpec(memory_space=pltpu.VMEM),
    )(pltpu.with_memory_space_constraint(parts, pltpu.VMEM))


def half_transform(left_rows, right_rows, block_ints, live_count):
    half_ints = jnp.einsum(
        "ikm,kmnq->kinq", left_rows, block_ints, preferred_element_type=jnp.float32
    )
    slot_ids = jnp.arange(block_ints.shape[0], dtype=jnp.int32)
    half_ints = jnp.where((slot_ids < live_count)[:, None, None, None], half_ints, 0.0).astype(
        jnp.bfloat16
    )
    return jnp.einsum("knv,kinq->ivq", right_rows, half_ints, preferred_element_type=jnp.float32)


def regrouping_device(ints, blk_atoms, blk_count, occ_coeff, vir_coeff, batch_ids):
    batch_size = batch_ids.shape[0]
    block_size = ints.shape[1]
    aux_local = ints.shape[3]
    picked = jnp.take(occ_coeff, batch_ids, axis=0)
    batch_coeff = lax.all_gather(picked, "occ", axis=1, tiled=True)
    atom_total = batch_coeff.shape[1] // block_size
    left_all = batch_coeff.reshape(batch_size, atom_total, block_size)[:, blk_atoms[:, 0], :]
    vir_local = vir_coeff.shape[1]
    right_all = vir_coeff.reshape(atom_total, block_size, vir_local)[blk_atoms[:, 1]]
    live_count = blk_count[0]
    summed = half_transform(left_all, right_all, ints, live_count)
    group_count = lax.axis_size("aux")
    vir_group = vir_local // group_count
    fitted = summed.astype(jnp.bfloat16).reshape(batch_size, group_count, vir_group, aux_local)
    regrouped = lax.all_to_all(
        lax.all_to_all(fitted, "aux", split_axis=1, concat_axis=3, tiled=True),
        "occ",
        split_axis=3,
        concat_axis=2,
        tiled=True,
    )
    group_rows = regrouped[:, 0]
    group_width = group_rows.shape[1]
    flat_rows = group_rows.reshape(batch_size * group_width, group_rows.shape[2])
    kept_rows = lax.psum_scatter(
        jnp.einsum("icq,xq->cix", group_rows, flat_rows, preferred_element_type=jnp.float32),
        "occ",
        scatter_dimension=0,
        tiled=True,
    )
    pair_ints = jnp.transpose(
        kept_rows.reshape(vir_group, batch_size, batch_size, group_width), (1, 0, 2, 3)
    )[:, None]
    return pair_ints


def on_device(ints, blk_atoms, blk_count, occ_coeff, vir_coeff, batch_ids):
    if lax.axis_size("occ") > 1:
        return regrouping_device(ints, blk_atoms, blk_count, occ_coeff, vir_coeff, batch_ids)
    batch = batch_ids.shape[0]
    groups = lax.axis_size("aux")
    group_width = vir_coeff.shape[1] // groups
    keep, send = partial_sums(ints, blk_atoms, blk_count, occ_coeff, vir_coeff, batch_ids, groups)
    partners = [(owner, owner ^ 1) for owner in range(groups)]
    parts = (keep + lax.ppermute(send, "aux", partners)).astype(jnp.bfloat16)
    parts = lax.all_to_all(parts, "aux", split_axis=0, concat_axis=0, tiled=True)
    total = total_sums(parts, batch, group_width)
    return total.reshape(batch, 1, group_width, batch, group_width)


def solution(mesh):
    in_specs = (
        P(None, None, None, "aux"),
        P("aux", None),
        P("aux"),
        P(None, "occ"),
        P(None, "occ"),
        P(),
    )
    out_specs = P(None, "aux", "occ", None, None)
    return jax.shard_map(
        on_device, mesh=mesh, in_specs=in_specs, out_specs=out_specs, check_vma=False
    )
```

```python
import functools

import jax
import jax.numpy as jnp
from jax import lax
from jax.experimental import pallas as pl
from jax.experimental.pallas import tpu as pltpu
from jax.sharding import PartitionSpec as P

LANES = 128
ROWS = 16
WINDOW = 3
CHUNKS = 1
PARTS = 2
EARLY = 1
PRIO = 1
TILE = 256


def device_order(count):
    order = []
    for plane in range(count // 8):
        chips = (0, 1, 3, 2) if plane % 2 == 0 else (2, 3, 1, 0)
        order += [plane * 8 + chip * 2 + core for chip in chips for core in range(2)]
    return order if len(order) == count else list(range(count))


def partial_kernel(
    group_width,
    places,
    atoms_hbm,
    count_hbm,
    ids_hbm,
    ints_hbm,
    occ_hbm,
    vir_hbm,
    keep_ref,
    send_ref,
    atoms_ref,
    count_ref,
    ids_ref,
    ints_buf,
    occ_buf,
    vir_buf,
    left_rows,
    left_big,
    right_rows,
    right_t,
    half_buf,
    fit_buf,
    small_sem,
    ints_sem,
    occ_sem,
    vir_sem,
):
    slots, depth, aux_local = ints_buf.shape
    batch = occ_buf.shape[0]
    groups = fit_buf.shape[0]
    virs = vir_buf.shape[1]
    owners = lax.axis_size("aux")
    me = lax.axis_index("aux")
    atom_total = occ_hbm.shape[1] // ROWS
    span = occ_hbm.shape[1] // owners
    span_atoms = span // ROWS
    window_atoms = left_big.shape[0]
    step = slots // CHUNKS
    part = aux_local // PARTS

    small_copies = [
        pltpu.make_async_copy(source, target, small_sem.at[s])
        for s, (source, target) in enumerate(
            ((ids_hbm, ids_ref), (atoms_hbm, atoms_ref), (count_hbm, count_ref))
        )
    ]
    for copy in small_copies:
        copy.start()
    starts = [pl.multiple_of(lax.rem(me + b, owners) * span, LANES) for b in range(WINDOW)]
    vir_copies = [
        pltpu.make_async_copy(
            vir_hbm.at[pl.ds(starts[b], span), :], vir_buf.at[pl.ds(b * span, span), :], vir_sem.at[b]
        )
        for b in range(WINDOW)
    ]
    for copy in vir_copies:
        copy.start()
    ints_copies = []
    for p in range(PARTS):
        for c in range(CHUNKS):
            block = (pl.ds(c * step, step), slice(None), pl.ds(p * part, part))
            ints_copies.append(
                pltpu.make_async_copy(ints_hbm.at[block], ints_buf.at[block], ints_sem.at[p, c])
            )
    for copy in ints_copies[:EARLY]:
        copy.start(priority=PRIO)
    small_copies[0].wait()
    occ_copies = []
    for i in range(batch):
        base = pl.multiple_of(ids_ref[i] & -ROWS, ROWS)
        for b in range(WINDOW):
            occ_copies.append(
                pltpu.make_async_copy(
                    occ_hbm.at[pl.ds(base, ROWS), pl.ds(starts[b], span)],
                    occ_buf.at[i, :, pl.ds(b * span, span)],
                    occ_sem.at[i, b],
                )
            )
    for copy in occ_copies:
        copy.start()
    for copy in ints_copies[EARLY:]:
        copy.start(priority=PRIO)
    for copy in small_copies[1:]:
        copy.wait()

    def near(slot, side):
        offset = atoms_ref[side, slot] - me * span_atoms
        offset = jnp.where(offset < 0, offset + atom_total, offset)
        return jnp.minimum(offset, window_atoms - 1)

    row_bits = ROWS.bit_length() - 1
    batch_bits = batch.bit_length() - 1
    quad = 4 * group_width
    wide = (quad, virs)
    row = lax.broadcasted_iota(jnp.int32, wide, 0)
    col = lax.broadcasted_iota(jnp.int32, wide, 1)
    low = (row >> 3) * group_width + (row & 7)
    high = ((row - 32) >> 2) * group_width + 8 + (row & 3)
    target = jnp.where(row < 32, low, high) - col
    spread = jnp.concatenate(
        [jnp.where(target == -start, 1.0, 0.0).astype(jnp.bfloat16) for start in range(0, virs, quad)],
        axis=0,
    )

    shape = (WINDOW * span, depth)
    row = lax.broadcasted_iota(jnp.int32, shape, 0) & (ROWS - 1)
    col = lax.broadcasted_iota(jnp.int32, shape, 1) >> row_bits
    repeat = jnp.where(row == col, 1.0, 0.0).astype(jnp.bfloat16)

    tall = (batch, batch * ROWS)
    row = lax.broadcasted_iota(jnp.int32, tall, 0)
    col = lax.broadcasted_iota(jnp.int32, tall, 1)
    wanted = jnp.zeros(tall, jnp.int32)
    for i in range(batch):
        wanted = jnp.where(row == i, i * ROWS + (ids_ref[i] & (ROWS - 1)), wanted)
    pick = jnp.where(col == wanted, 1.0, 0.0).astype(jnp.bfloat16)

    for copy in vir_copies:
        copy.wait()
    for k in range(slots):
        rows = vir_buf[pl.ds(pl.multiple_of(near(k, 1) * ROWS, ROWS), ROWS), :]
        live = jnp.where(k < count_ref[0], 1.0, 0.0).astype(jnp.bfloat16)
        right_rows[k * ROWS : (k + 1) * ROWS, :] = rows * live
    right_t[...] = lax.dot_general(
        spread, right_rows[...], (((1,), (1,)), ((), ())), preferred_element_type=jnp.float32
    ).astype(jnp.bfloat16)

    for copy in occ_copies:
        copy.wait()
    picked = jnp.dot(
        pick, occ_buf[...].reshape(batch * ROWS, WINDOW * span), preferred_element_type=jnp.float32
    )
    picked = jnp.concatenate([picked] * window_atoms, axis=0)
    row = lax.broadcasted_iota(jnp.int32, picked.shape, 0) >> batch_bits
    col = lax.broadcasted_iota(jnp.int32, picked.shape, 1) >> row_bits
    picked = jnp.where(row == col, picked, 0.0).astype(jnp.bfloat16)
    left_rows[...] = jnp.dot(picked, repeat, preferred_element_type=jnp.float32)

    shape = (ROWS, depth)
    diagonal = lax.broadcasted_iota(jnp.int32, shape, 0) == (
        lax.broadcasted_iota(jnp.int32, shape, 1) & (ROWS - 1)
    )
    for a in range(window_atoms):
        rows = left_rows[a * batch : (a + 1) * batch, :]
        for i in range(batch):
            left_big[a, i * ROWS : (i + 1) * ROWS, :] = jnp.where(
                diagonal, rows[i : i + 1, :], 0.0
            ).astype(jnp.bfloat16)

    for p in range(PARTS):
        cols = slice(p * part, (p + 1) * part)
        for c in range(CHUNKS):
            ints_copies[p * CHUNKS + c].wait()
            for k in range(c * step, (c + 1) * step):
                half = jnp.dot(
                    left_big[near(k, 0)], ints_buf[k, :, cols], preferred_element_type=jnp.float32
                ).astype(jnp.bfloat16)
                for i in range(batch):
                    half_buf[i, k * ROWS : (k + 1) * ROWS, cols] = half[i * ROWS : (i + 1) * ROWS, :]
        for i in range(batch):
            for q in range(p * part, (p + 1) * part, TILE):
                fitted = jnp.dot(
                    right_t[...], half_buf[i, :, q : q + TILE], preferred_element_type=jnp.float32
                )
                for g in range(groups):
                    start = g // 4 * quad
                    low = fitted[start + g % 4 * 8 : start + g % 4 * 8 + 8, :]
                    start += 32 + g % 4 // 2 * 8
                    high = fitted[start : start + 8, :]
                    if g % 2 == 1:
                        high = pltpu.roll(high, 4, 0)
                    fit_buf[g, i * ROWS : (i + 1) * ROWS, q : q + TILE] = jnp.concatenate(
                        [low, high], axis=0
                    ).astype(jnp.bfloat16)

    upper = batch // 2 * ROWS
    shape = (upper, LANES)
    row = lax.broadcasted_iota(jnp.int32, shape, 0)
    col = lax.broadcasted_iota(jnp.int32, shape, 1)
    from_below = (col < upper) & (col > row)
    top_half = lax.broadcasted_iota(jnp.int32, (8, LANES), 0) < 4
    own = lax.rem(me, 2)
    high = batch * ROWS
    for first_group in range(0, groups, 2):
        both = fit_buf[first_group : first_group + 2].reshape(2 * high, aux_local)
        grams = lax.dot_general(
            both, both, (((1,), (1,)), ((), ())), preferred_element_type=jnp.float32
        )
        for g in range(2):
            gram = grams[g * high : (g + 1) * high, g * high : (g + 1) * high]
            below = pltpu.roll(gram[upper:, :], upper + 1, 1)
            packed = jnp.where(from_below, below, gram[:upper, :])
            halves = []
            for i in range(0, batch // 2, 2):
                first = packed[i * ROWS : (i + 1) * ROWS, :]
                second = packed[(i + 1) * ROWS : (i + 2) * ROWS, :]
                mixed = jnp.where(top_half, first[8:, :], pltpu.roll(second[8:, :], 4, 0))
                halves.append(jnp.concatenate([first[:8, :], mixed, second[:8, :]], axis=0))
            keep_ref[places[first_group + g]] = jnp.where(own == 0, halves[0], halves[1])
            send_ref[places[first_group + g]] = jnp.where(own == 0, halves[1], halves[0])


def in_place(operand):
    return pltpu.with_memory_space_constraint(operand, pltpu.HBM)


def partial_sums(ints, blk_atoms, blk_count, occ_coeff, vir_coeff, batch_ids, places):
    groups = len(places)
    slots, block, _, aux_local = ints.shape
    batch = batch_ids.shape[0]
    virs = vir_coeff.shape[1]
    basis = occ_coeff.shape[1]
    span = basis // groups
    window_atoms = (WINDOW - 1) * span // block + 1
    depth = block * block
    group_width = virs // groups
    far = pl.BlockSpec(memory_space=pltpu.HBM)
    result = jax.ShapeDtypeStruct((groups, batch // 4 * group_width, LANES), jnp.float32)
    return pl.pallas_call(
        functools.partial(partial_kernel, group_width, places),
        out_shape=(result, result),
        in_specs=[far] * 6,
        out_specs=[pl.BlockSpec(memory_space=pltpu.VMEM)] * 2,
        scratch_shapes=[
            pltpu.SMEM((2, slots), jnp.int32),
            pltpu.SMEM((1,), jnp.int32),
            pltpu.SMEM((batch,), jnp.int32),
            pltpu.VMEM((slots, depth, aux_local), jnp.bfloat16),
            pltpu.VMEM((batch, ROWS, WINDOW * span), jnp.bfloat16),
            pltpu.VMEM((WINDOW * span, virs), jnp.bfloat16),
            pltpu.VMEM((window_atoms * batch, depth), jnp.float32),
            pltpu.VMEM((window_atoms, batch * ROWS, depth), jnp.bfloat16),
            pltpu.VMEM((slots * ROWS, virs), jnp.bfloat16),
            pltpu.VMEM((virs, slots * ROWS), jnp.bfloat16),
            pltpu.VMEM((batch, slots * ROWS, aux_local), jnp.bfloat16),
            pltpu.VMEM((groups, batch * ROWS, aux_local), jnp.bfloat16),
            pltpu.SemaphoreType.DMA((3,)),
            pltpu.SemaphoreType.DMA((PARTS, CHUNKS)),
            pltpu.SemaphoreType.DMA((batch, WINDOW)),
            pltpu.SemaphoreType.DMA((WINDOW,)),
        ],
        compiler_params=pltpu.CompilerParams(vmem_limit_bytes=40 * 1024 * 1024),
    )(
        in_place(blk_atoms.T),
        blk_count,
        in_place(batch_ids),
        in_place(ints.reshape(slots, depth, aux_local)),
        in_place(occ_coeff),
        in_place(vir_coeff),
    )


def total_kernel(group_width, batch, parts_ref, out_ref):
    owners, rows, _ = parts_ref.shape
    total = jnp.sum(
        parts_ref[...].astype(jnp.float32).reshape(owners // 2, 2 * rows, LANES), axis=0
    )
    upper = batch // 2 * ROWS
    top_half = lax.broadcasted_iota(jnp.int32, (8, LANES), 0) < 4
    pieces = []
    for i in range(0, batch // 2, 2):
        first, mixed, second = (
            total[(3 * (i // 2) + s) * 8 : (3 * (i // 2) + s + 1) * 8, :] for s in range(3)
        )
        pieces += [
            first,
            jnp.where(top_half, mixed, 0.0),
            second,
            jnp.where(top_half, pltpu.roll(mixed, 4, 0), 0.0),
        ]
    above = jnp.concatenate(pieces, axis=0)
    both = jnp.concatenate([above, pltpu.roll(above, upper - 1, 1)], axis=0)
    shape = (2 * upper, 2 * upper)
    row = lax.broadcasted_iota(jnp.int32, shape, 0)
    col = lax.broadcasted_iota(jnp.int32, shape, 1)
    direct = ((row < upper) & ((col >= upper) | (col <= row))) | ((row >= upper) & (col >= row))
    whole = jnp.where(direct, both, both.T)
    for i in range(batch):
        for c in range(0, group_width, 8):
            rows = whole[i * ROWS + c : i * ROWS + c + 8, :]
            count = min(8, group_width - c)
            for j in range(batch):
                moved = rows if j == 0 else pltpu.roll(rows, LANES - j * ROWS, 1)
                start = (i * group_width + c) * batch + j
                out_ref[pl.ds(start, count, stride=batch), :] = moved[:count, :group_width]


def total_sums(parts, batch, group_width):
    return pl.pallas_call(
        functools.partial(total_kernel, group_width, batch),
        out_shape=jax.ShapeDtypeStruct((batch * group_width * batch, group_width), jnp.float32),
        in_specs=[pl.BlockSpec(memory_space=pltpu.VMEM)],
        out_specs=pl.BlockSpec(memory_space=pltpu.VMEM),
    )(pltpu.with_memory_space_constraint(parts, pltpu.VMEM))


def half_transform(left_rows, right_rows, block_ints, live_count):
    half_ints = jnp.einsum(
        "ikm,kmnq->kinq", left_rows, block_ints, preferred_element_type=jnp.float32
    )
    slot_ids = jnp.arange(block_ints.shape[0], dtype=jnp.int32)
    half_ints = jnp.where((slot_ids < live_count)[:, None, None, None], half_ints, 0.0).astype(
        jnp.bfloat16
    )
    return jnp.einsum("knv,kinq->ivq", right_rows, half_ints, preferred_element_type=jnp.float32)


def regrouping_device(ints, blk_atoms, blk_count, occ_coeff, vir_coeff, batch_ids):
    batch_size = batch_ids.shape[0]
    block_size = ints.shape[1]
    aux_local = ints.shape[3]
    picked = jnp.take(occ_coeff, batch_ids, axis=0)
    batch_coeff = lax.all_gather(picked, "occ", axis=1, tiled=True)
    atom_total = batch_coeff.shape[1] // block_size
    left_all = batch_coeff.reshape(batch_size, atom_total, block_size)[:, blk_atoms[:, 0], :]
    vir_local = vir_coeff.shape[1]
    right_all = vir_coeff.reshape(atom_total, block_size, vir_local)[blk_atoms[:, 1]]
    live_count = blk_count[0]
    summed = half_transform(left_all, right_all, ints, live_count)
    group_count = lax.axis_size("aux")
    vir_group = vir_local // group_count
    fitted = summed.astype(jnp.bfloat16).reshape(batch_size, group_count, vir_group, aux_local)
    regrouped = lax.all_to_all(
        lax.all_to_all(fitted, "aux", split_axis=1, concat_axis=3, tiled=True),
        "occ",
        split_axis=3,
        concat_axis=2,
        tiled=True,
    )
    group_rows = regrouped[:, 0]
    group_width = group_rows.shape[1]
    flat_rows = group_rows.reshape(batch_size * group_width, group_rows.shape[2])
    kept_rows = lax.psum_scatter(
        jnp.einsum("icq,xq->cix", group_rows, flat_rows, preferred_element_type=jnp.float32),
        "occ",
        scatter_dimension=0,
        tiled=True,
    )
    pair_ints = jnp.transpose(
        kept_rows.reshape(vir_group, batch_size, batch_size, group_width), (1, 0, 2, 3)
    )[:, None]
    return pair_ints


def on_device(ints, blk_atoms, blk_count, occ_coeff, vir_coeff, batch_ids):
    if lax.axis_size("occ") > 1:
        return regrouping_device(ints, blk_atoms, blk_count, occ_coeff, vir_coeff, batch_ids)
    batch = batch_ids.shape[0]
    groups = lax.axis_size("aux")
    group_width = vir_coeff.shape[1] // groups
    order = device_order(groups)
    places = [order.index(group) for group in range(groups)]
    keep, send = partial_sums(ints, blk_atoms, blk_count, occ_coeff, vir_coeff, batch_ids, places)
    partners = [(owner, owner ^ 1) for owner in range(groups)]
    parts = (keep + lax.ppermute(send, "aux", partners)).astype(jnp.bfloat16)
    parts = lax.all_to_all(
        parts, "aux", split_axis=0, concat_axis=0, tiled=True, axis_index_groups=[order]
    )
    total = total_sums(parts, batch, group_width)
    return total.reshape(batch, 1, group_width, batch, group_width)


def solution(mesh):
    in_specs = (
        P(None, None, None, "aux"),
        P("aux", None),
        P("aux"),
        P(None, "occ"),
        P(None, "occ"),
        P(),
    )
    out_specs = P(None, "aux", "occ", None, None)
    return jax.shard_map(
        on_device, mesh=mesh, in_specs=in_specs, out_specs=out_specs, check_vma=False
    )
```

```python
import functools

import jax
import jax.numpy as jnp
from jax import lax
from jax.experimental import pallas as pl
from jax.experimental.pallas import tpu as pltpu
from jax.sharding import PartitionSpec as P

LANES = 128
ROWS = 16
WINDOW = 3
CHUNKS = 1
PARTS = 2
EARLY = 1
PRIO = 1
TILE = 256


def device_order(count):
    order = []
    for plane in range(count // 8):
        chips = (0, 1, 3, 2) if plane % 2 == 0 else (2, 3, 1, 0)
        order += [plane * 8 + chip * 2 + core for chip in chips for core in range(2)]
    return order if len(order) == count else list(range(count))


def partial_kernel(
    group_width,
    places,
    atoms_hbm,
    count_hbm,
    ids_hbm,
    ints_hbm,
    occ_hbm,
    vir_hbm,
    keep_ref,
    send_ref,
    atoms_ref,
    count_ref,
    ids_ref,
    ints_buf,
    occ_buf,
    vir_buf,
    left_rows,
    left_big,
    right_rows,
    right_t,
    half_buf,
    fit_buf,
    small_sem,
    ints_sem,
    occ_sem,
    vir_sem,
):
    slots, depth, aux_local = ints_buf.shape
    batch = occ_buf.shape[0]
    groups = fit_buf.shape[0]
    virs = vir_buf.shape[1]
    owners = lax.axis_size("aux")
    me = lax.axis_index("aux")
    atom_total = occ_hbm.shape[1] // ROWS
    span = occ_hbm.shape[1] // owners
    span_atoms = span // ROWS
    window_atoms = left_big.shape[0]
    step = slots // CHUNKS
    part = aux_local // PARTS

    small_copies = [
        pltpu.make_async_copy(source, target, small_sem.at[s])
        for s, (source, target) in enumerate(
            ((ids_hbm, ids_ref), (atoms_hbm, atoms_ref), (count_hbm, count_ref))
        )
    ]
    for copy in small_copies:
        copy.start()
    starts = [pl.multiple_of(lax.rem(me + b, owners) * span, LANES) for b in range(WINDOW)]
    vir_copies = [
        pltpu.make_async_copy(
            vir_hbm.at[pl.ds(starts[b], span), :], vir_buf.at[pl.ds(b * span, span), :], vir_sem.at[b]
        )
        for b in range(WINDOW)
    ]
    for copy in vir_copies:
        copy.start()
    ints_copies = []
    for p in range(PARTS):
        for c in range(CHUNKS):
            block = (pl.ds(c * step, step), slice(None), pl.ds(p * part, part))
            ints_copies.append(
                pltpu.make_async_copy(ints_hbm.at[block], ints_buf.at[block], ints_sem.at[p, c])
            )
    for copy in ints_copies[:EARLY]:
        copy.start(priority=PRIO)
    small_copies[0].wait()
    occ_copies = []
    for i in range(batch):
        base = pl.multiple_of(ids_ref[i] & -ROWS, ROWS)
        for b in range(WINDOW):
            occ_copies.append(
                pltpu.make_async_copy(
                    occ_hbm.at[pl.ds(base, ROWS), pl.ds(starts[b], span)],
                    occ_buf.at[i, :, pl.ds(b * span, span)],
                    occ_sem.at[i, b],
                )
            )
    for copy in occ_copies:
        copy.start()
    for copy in ints_copies[EARLY:]:
        copy.start(priority=PRIO)
    for copy in small_copies[1:]:
        copy.wait()

    def near(slot, side):
        offset = atoms_ref[side, slot] - me * span_atoms
        offset = jnp.where(offset < 0, offset + atom_total, offset)
        return jnp.minimum(offset, window_atoms - 1)

    row_bits = ROWS.bit_length() - 1
    batch_bits = batch.bit_length() - 1
    quad = 4 * group_width
    wide = (quad, virs)
    row = lax.broadcasted_iota(jnp.int32, wide, 0)
    col = lax.broadcasted_iota(jnp.int32, wide, 1)
    low = (row >> 3) * group_width + (row & 7)
    high = ((row - 32) >> 2) * group_width + 8 + (row & 3)
    target = jnp.where(row < 32, low, high) - col
    spread = jnp.concatenate(
        [jnp.where(target == -start, 1.0, 0.0).astype(jnp.bfloat16) for start in range(0, virs, quad)],
        axis=0,
    )

    shape = (WINDOW * span, depth)
    row = lax.broadcasted_iota(jnp.int32, shape, 0) & (ROWS - 1)
    col = lax.broadcasted_iota(jnp.int32, shape, 1) >> row_bits
    repeat = jnp.where(row == col, 1.0, 0.0).astype(jnp.bfloat16)

    tall = (batch, batch * ROWS)
    row = lax.broadcasted_iota(jnp.int32, tall, 0)
    col = lax.broadcasted_iota(jnp.int32, tall, 1)
    wanted = jnp.zeros(tall, jnp.int32)
    for i in range(batch):
        wanted = jnp.where(row == i, i * ROWS + (ids_ref[i] & (ROWS - 1)), wanted)
    pick = jnp.where(col == wanted, 1.0, 0.0).astype(jnp.bfloat16)

    for copy in vir_copies:
        copy.wait()
    for k in range(slots):
        rows = vir_buf[pl.ds(pl.multiple_of(near(k, 1) * ROWS, ROWS), ROWS), :]
        live = jnp.where(k < count_ref[0], 1.0, 0.0).astype(jnp.bfloat16)
        right_rows[k * ROWS : (k + 1) * ROWS, :] = rows * live
    right_t[...] = lax.dot_general(
        spread, right_rows[...], (((1,), (1,)), ((), ())), preferred_element_type=jnp.float32
    ).astype(jnp.bfloat16)

    for copy in occ_copies:
        copy.wait()
    picked = jnp.dot(
        pick, occ_buf[...].reshape(batch * ROWS, WINDOW * span), preferred_element_type=jnp.float32
    )
    picked = jnp.concatenate([picked] * window_atoms, axis=0)
    row = lax.broadcasted_iota(jnp.int32, picked.shape, 0) >> batch_bits
    col = lax.broadcasted_iota(jnp.int32, picked.shape, 1) >> row_bits
    picked = jnp.where(row == col, picked, 0.0).astype(jnp.bfloat16)
    left_rows[...] = jnp.dot(picked, repeat, preferred_element_type=jnp.float32)

    shape = (ROWS, depth)
    diagonal = lax.broadcasted_iota(jnp.int32, shape, 0) == (
        lax.broadcasted_iota(jnp.int32, shape, 1) & (ROWS - 1)
    )
    for a in range(window_atoms):
        rows = left_rows[a * batch : (a + 1) * batch, :]
        for i in range(batch):
            left_big[a, i * ROWS : (i + 1) * ROWS, :] = jnp.where(
                diagonal, rows[i : i + 1, :], 0.0
            ).astype(jnp.bfloat16)

    for p in range(PARTS):
        cols = slice(p * part, (p + 1) * part)
        for c in range(CHUNKS):
            ints_copies[p * CHUNKS + c].wait()
            for k in range(c * step, (c + 1) * step):
                half = jnp.dot(
                    left_big[near(k, 0)], ints_buf[k, :, cols], preferred_element_type=jnp.float32
                ).astype(jnp.bfloat16)
                for i in range(batch):
                    half_buf[i, k * ROWS : (k + 1) * ROWS, cols] = half[i * ROWS : (i + 1) * ROWS, :]
        for i in range(batch):
            for q in range(p * part, (p + 1) * part, TILE):
                fitted = jnp.dot(
                    right_t[...], half_buf[i, :, q : q + TILE], preferred_element_type=jnp.float32
                )
                for g in range(groups):
                    start = g // 4 * quad
                    low = fitted[start + g % 4 * 8 : start + g % 4 * 8 + 8, :]
                    start += 32 + g % 4 // 2 * 8
                    high = fitted[start : start + 8, :]
                    if g % 2 == 1:
                        high = pltpu.roll(high, 4, 0)
                    fit_buf[g, i * ROWS : (i + 1) * ROWS, q : q + TILE] = jnp.concatenate(
                        [low, high], axis=0
                    ).astype(jnp.bfloat16)

    upper = batch // 2 * ROWS
    shape = (upper, LANES)
    row = lax.broadcasted_iota(jnp.int32, shape, 0)
    col = lax.broadcasted_iota(jnp.int32, shape, 1)
    from_below = (col < upper) & (col > row)
    top_half = lax.broadcasted_iota(jnp.int32, (8, LANES), 0) < 4
    own = lax.rem(me, 2)
    high = batch * ROWS
    for first_group in range(0, groups, 2):
        both = fit_buf[first_group : first_group + 2].reshape(2 * high, aux_local)
        grams = lax.dot_general(
            both, both, (((1,), (1,)), ((), ())), preferred_element_type=jnp.float32
        )
        for g in range(2):
            gram = grams[g * high : (g + 1) * high, g * high : (g + 1) * high]
            below = pltpu.roll(gram[upper:, :], upper + 1, 1)
            packed = jnp.where(from_below, below, gram[:upper, :])
            halves = []
            for i in range(0, batch // 2, 2):
                first = packed[i * ROWS : (i + 1) * ROWS, :]
                second = packed[(i + 1) * ROWS : (i + 2) * ROWS, :]
                mixed = jnp.where(top_half, first[8:, :], pltpu.roll(second[8:, :], 4, 0))
                halves.append(jnp.concatenate([first[:8, :], mixed, second[:8, :]], axis=0))
            keep_ref[places[first_group + g]] = jnp.where(own == 0, halves[0], halves[1])
            send_ref[places[first_group + g]] = jnp.where(own == 0, halves[1], halves[0]).astype(
                jnp.bfloat16
            )


def in_place(operand):
    return pltpu.with_memory_space_constraint(operand, pltpu.HBM)


def partial_sums(ints, blk_atoms, blk_count, occ_coeff, vir_coeff, batch_ids, places):
    groups = len(places)
    slots, block, _, aux_local = ints.shape
    batch = batch_ids.shape[0]
    virs = vir_coeff.shape[1]
    basis = occ_coeff.shape[1]
    span = basis // groups
    window_atoms = (WINDOW - 1) * span // block + 1
    depth = block * block
    group_width = virs // groups
    far = pl.BlockSpec(memory_space=pltpu.HBM)
    shape = (groups, batch // 4 * group_width, LANES)
    return pl.pallas_call(
        functools.partial(partial_kernel, group_width, places),
        out_shape=(
            jax.ShapeDtypeStruct(shape, jnp.float32),
            jax.ShapeDtypeStruct(shape, jnp.bfloat16),
        ),
        in_specs=[far] * 6,
        out_specs=[pl.BlockSpec(memory_space=pltpu.VMEM)] * 2,
        scratch_shapes=[
            pltpu.SMEM((2, slots), jnp.int32),
            pltpu.SMEM((1,), jnp.int32),
            pltpu.SMEM((batch,), jnp.int32),
            pltpu.VMEM((slots, depth, aux_local), jnp.bfloat16),
            pltpu.VMEM((batch, ROWS, WINDOW * span), jnp.bfloat16),
            pltpu.VMEM((WINDOW * span, virs), jnp.bfloat16),
            pltpu.VMEM((window_atoms * batch, depth), jnp.float32),
            pltpu.VMEM((window_atoms, batch * ROWS, depth), jnp.bfloat16),
            pltpu.VMEM((slots * ROWS, virs), jnp.bfloat16),
            pltpu.VMEM((virs, slots * ROWS), jnp.bfloat16),
            pltpu.VMEM((batch, slots * ROWS, aux_local), jnp.bfloat16),
            pltpu.VMEM((groups, batch * ROWS, aux_local), jnp.bfloat16),
            pltpu.SemaphoreType.DMA((3,)),
            pltpu.SemaphoreType.DMA((PARTS, CHUNKS)),
            pltpu.SemaphoreType.DMA((batch, WINDOW)),
            pltpu.SemaphoreType.DMA((WINDOW,)),
        ],
        compiler_params=pltpu.CompilerParams(vmem_limit_bytes=40 * 1024 * 1024),
    )(
        in_place(blk_atoms.T),
        blk_count,
        in_place(batch_ids),
        in_place(ints.reshape(slots, depth, aux_local)),
        in_place(occ_coeff),
        in_place(vir_coeff),
    )


def total_kernel(group_width, batch, parts_ref, out_ref):
    owners, rows, _ = parts_ref.shape
    total = jnp.sum(
        parts_ref[...].astype(jnp.float32).reshape(owners // 2, 2 * rows, LANES), axis=0
    )
    upper = batch // 2 * ROWS
    top_half = lax.broadcasted_iota(jnp.int32, (8, LANES), 0) < 4
    pieces = []
    for i in range(0, batch // 2, 2):
        first, mixed, second = (
            total[(3 * (i // 2) + s) * 8 : (3 * (i // 2) + s + 1) * 8, :] for s in range(3)
        )
        pieces += [
            first,
            jnp.where(top_half, mixed, 0.0),
            second,
            jnp.where(top_half, pltpu.roll(mixed, 4, 0), 0.0),
        ]
    above = jnp.concatenate(pieces, axis=0)
    both = jnp.concatenate([above, pltpu.roll(above, upper - 1, 1)], axis=0)
    shape = (2 * upper, 2 * upper)
    row = lax.broadcasted_iota(jnp.int32, shape, 0)
    col = lax.broadcasted_iota(jnp.int32, shape, 1)
    direct = ((row < upper) & ((col >= upper) | (col <= row))) | ((row >= upper) & (col >= row))
    whole = jnp.where(direct, both, both.T)
    for i in range(batch):
        for c in range(0, group_width, 8):
            rows = whole[i * ROWS + c : i * ROWS + c + 8, :]
            count = min(8, group_width - c)
            for j in range(batch):
                moved = rows if j == 0 else pltpu.roll(rows, LANES - j * ROWS, 1)
                start = (i * group_width + c) * batch + j
                out_ref[pl.ds(start, count, stride=batch), :] = moved[:count, :group_width]


def total_sums(parts, batch, group_width):
    return pl.pallas_call(
        functools.partial(total_kernel, group_width, batch),
        out_shape=jax.ShapeDtypeStruct((batch * group_width * batch, group_width), jnp.float32),
        in_specs=[pl.BlockSpec(memory_space=pltpu.VMEM)],
        out_specs=pl.BlockSpec(memory_space=pltpu.VMEM),
    )(pltpu.with_memory_space_constraint(parts, pltpu.VMEM))


def half_transform(left_rows, right_rows, block_ints, live_count):
    half_ints = jnp.einsum(
        "ikm,kmnq->kinq", left_rows, block_ints, preferred_element_type=jnp.float32
    )
    slot_ids = jnp.arange(block_ints.shape[0], dtype=jnp.int32)
    half_ints = jnp.where((slot_ids < live_count)[:, None, None, None], half_ints, 0.0).astype(
        jnp.bfloat16
    )
    return jnp.einsum("knv,kinq->ivq", right_rows, half_ints, preferred_element_type=jnp.float32)


def regrouping_device(ints, blk_atoms, blk_count, occ_coeff, vir_coeff, batch_ids):
    batch_size = batch_ids.shape[0]
    block_size = ints.shape[1]
    aux_local = ints.shape[3]
    picked = jnp.take(occ_coeff, batch_ids, axis=0)
    batch_coeff = lax.all_gather(picked, "occ", axis=1, tiled=True)
    atom_total = batch_coeff.shape[1] // block_size
    left_all = batch_coeff.reshape(batch_size, atom_total, block_size)[:, blk_atoms[:, 0], :]
    vir_local = vir_coeff.shape[1]
    right_all = vir_coeff.reshape(atom_total, block_size, vir_local)[blk_atoms[:, 1]]
    live_count = blk_count[0]
    summed = half_transform(left_all, right_all, ints, live_count)
    group_count = lax.axis_size("aux")
    vir_group = vir_local // group_count
    fitted = summed.astype(jnp.bfloat16).reshape(batch_size, group_count, vir_group, aux_local)
    regrouped = lax.all_to_all(
        lax.all_to_all(fitted, "aux", split_axis=1, concat_axis=3, tiled=True),
        "occ",
        split_axis=3,
        concat_axis=2,
        tiled=True,
    )
    group_rows = regrouped[:, 0]
    group_width = group_rows.shape[1]
    flat_rows = group_rows.reshape(batch_size * group_width, group_rows.shape[2])
    kept_rows = lax.psum_scatter(
        jnp.einsum("icq,xq->cix", group_rows, flat_rows, preferred_element_type=jnp.float32),
        "occ",
        scatter_dimension=0,
        tiled=True,
    )
    pair_ints = jnp.transpose(
        kept_rows.reshape(vir_group, batch_size, batch_size, group_width), (1, 0, 2, 3)
    )[:, None]
    return pair_ints


def on_device(ints, blk_atoms, blk_count, occ_coeff, vir_coeff, batch_ids):
    if lax.axis_size("occ") > 1:
        return regrouping_device(ints, blk_atoms, blk_count, occ_coeff, vir_coeff, batch_ids)
    batch = batch_ids.shape[0]
    groups = lax.axis_size("aux")
    group_width = vir_coeff.shape[1] // groups
    order = device_order(groups)
    places = [order.index(group) for group in range(groups)]
    keep, send = partial_sums(ints, blk_atoms, blk_count, occ_coeff, vir_coeff, batch_ids, places)
    partners = [(owner, owner ^ 1) for owner in range(groups)]
    parts = (keep + lax.ppermute(send, "aux", partners)).astype(jnp.bfloat16)
    parts = lax.all_to_all(
        parts, "aux", split_axis=0, concat_axis=0, tiled=True, axis_index_groups=[order]
    )
    total = total_sums(parts, batch, group_width)
    return total.reshape(batch, 1, group_width, batch, group_width)


def solution(mesh):
    in_specs = (
        P(None, None, None, "aux"),
        P("aux", None),
        P("aux"),
        P(None, "occ"),
        P(None, "occ"),
        P(),
    )
    out_specs = P(None, "aux", "occ", None, None)
    return jax.shard_map(
        on_device, mesh=mesh, in_specs=in_specs, out_specs=out_specs, check_vma=False
    )
```

```python
import functools

import jax
import jax.numpy as jnp
from jax import lax
from jax.experimental import pallas as pl
from jax.experimental.pallas import tpu as pltpu
from jax.sharding import PartitionSpec as P

LANES = 128
ROWS = 16
WINDOW = 3
CHUNKS = 1
PARTS = 2
EARLY = 1
PRIO = 1
TILE = 256


def device_order(count):
    order = []
    for plane in range(count // 8):
        chips = (0, 1, 3, 2) if plane % 2 == 0 else (2, 3, 1, 0)
        order += [plane * 8 + chip * 2 + core for chip in chips for core in range(2)]
    return order if len(order) == count else list(range(count))


def partial_kernel(
    group_width,
    places,
    atoms_hbm,
    count_ref,
    ids_hbm,
    ints_hbm,
    occ_hbm,
    vir_hbm,
    keep_ref,
    send_ref,
    atoms_ref,
    ids_ref,
    ints_buf,
    occ_buf,
    vir_buf,
    left_rows,
    left_big,
    right_rows,
    right_t,
    half_buf,
    fit_buf,
    small_sem,
    ints_sem,
    occ_sem,
    vir_sem,
):
    slots, depth, aux_local = ints_buf.shape
    batch = occ_buf.shape[0]
    groups = fit_buf.shape[0]
    virs = vir_buf.shape[1]
    owners = lax.axis_size("aux")
    me = lax.axis_index("aux")
    atom_total = occ_hbm.shape[1] // ROWS
    span = occ_hbm.shape[1] // owners
    span_atoms = span // ROWS
    window_atoms = left_big.shape[0]
    step = slots // CHUNKS
    part = aux_local // PARTS

    small_copies = [
        pltpu.make_async_copy(source, target, small_sem.at[s])
        for s, (source, target) in enumerate(
            ((ids_hbm, ids_ref), (atoms_hbm, atoms_ref))
        )
    ]
    for copy in small_copies:
        copy.start()
    starts = [pl.multiple_of(lax.rem(me + b, owners) * span, LANES) for b in range(WINDOW)]
    vir_copies = [
        pltpu.make_async_copy(
            vir_hbm.at[pl.ds(starts[b], span), :], vir_buf.at[pl.ds(b * span, span), :], vir_sem.at[b]
        )
        for b in range(WINDOW)
    ]
    for copy in vir_copies:
        copy.start()
    ints_copies = []
    for p in range(PARTS):
        for c in range(CHUNKS):
            block = (pl.ds(c * step, step), slice(None), pl.ds(p * part, part))
            ints_copies.append(
                pltpu.make_async_copy(ints_hbm.at[block], ints_buf.at[block], ints_sem.at[p, c])
            )
    for copy in ints_copies[:EARLY]:
        copy.start(priority=PRIO)
    small_copies[0].wait()
    occ_copies = []
    for i in range(batch):
        base = pl.multiple_of(ids_ref[i] & -ROWS, ROWS)
        for b in range(WINDOW):
            occ_copies.append(
                pltpu.make_async_copy(
                    occ_hbm.at[pl.ds(base, ROWS), pl.ds(starts[b], span)],
                    occ_buf.at[i, :, pl.ds(b * span, span)],
                    occ_sem.at[i, b],
                )
            )
    for copy in occ_copies:
        copy.start()
    for copy in ints_copies[EARLY:]:
        copy.start(priority=PRIO)
    for copy in small_copies[1:]:
        copy.wait()

    def near(slot, side):
        offset = atoms_ref[side, slot] - me * span_atoms
        offset = jnp.where(offset < 0, offset + atom_total, offset)
        return jnp.minimum(offset, window_atoms - 1)

    row_bits = ROWS.bit_length() - 1
    batch_bits = batch.bit_length() - 1
    quad = 4 * group_width
    wide = (quad, virs)
    row = lax.broadcasted_iota(jnp.int32, wide, 0)
    col = lax.broadcasted_iota(jnp.int32, wide, 1)
    low = (row >> 3) * group_width + (row & 7)
    high = ((row - 32) >> 2) * group_width + 8 + (row & 3)
    target = jnp.where(row < 32, low, high) - col
    spread = jnp.concatenate(
        [jnp.where(target == -start, 1.0, 0.0).astype(jnp.bfloat16) for start in range(0, virs, quad)],
        axis=0,
    )

    shape = (WINDOW * span, depth)
    row = lax.broadcasted_iota(jnp.int32, shape, 0) & (ROWS - 1)
    col = lax.broadcasted_iota(jnp.int32, shape, 1) >> row_bits
    repeat = jnp.where(row == col, 1.0, 0.0).astype(jnp.bfloat16)

    tall = (batch, batch * ROWS)
    row = lax.broadcasted_iota(jnp.int32, tall, 0)
    col = lax.broadcasted_iota(jnp.int32, tall, 1)
    wanted = jnp.zeros(tall, jnp.int32)
    for i in range(batch):
        wanted = jnp.where(row == i, i * ROWS + (ids_ref[i] & (ROWS - 1)), wanted)
    pick = jnp.where(col == wanted, 1.0, 0.0).astype(jnp.bfloat16)

    for copy in vir_copies:
        copy.wait()
    for k in range(slots):
        rows = vir_buf[pl.ds(pl.multiple_of(near(k, 1) * ROWS, ROWS), ROWS), :]
        live = jnp.where(k < count_ref[0], 1.0, 0.0).astype(jnp.bfloat16)
        right_rows[k * ROWS : (k + 1) * ROWS, :] = rows * live
    right_t[...] = lax.dot_general(
        spread, right_rows[...], (((1,), (1,)), ((), ())), preferred_element_type=jnp.float32
    ).astype(jnp.bfloat16)

    for copy in occ_copies:
        copy.wait()
    picked = jnp.dot(
        pick, occ_buf[...].reshape(batch * ROWS, WINDOW * span), preferred_element_type=jnp.float32
    )
    picked = jnp.concatenate([picked] * window_atoms, axis=0)
    row = lax.broadcasted_iota(jnp.int32, picked.shape, 0) >> batch_bits
    col = lax.broadcasted_iota(jnp.int32, picked.shape, 1) >> row_bits
    picked = jnp.where(row == col, picked, 0.0).astype(jnp.bfloat16)
    left_rows[...] = jnp.dot(picked, repeat, preferred_element_type=jnp.float32)

    shape = (ROWS, depth)
    diagonal = lax.broadcasted_iota(jnp.int32, shape, 0) == (
        lax.broadcasted_iota(jnp.int32, shape, 1) & (ROWS - 1)
    )
    for a in range(window_atoms):
        rows = left_rows[a * batch : (a + 1) * batch, :]
        for i in range(batch):
            left_big[a, i * ROWS : (i + 1) * ROWS, :] = jnp.where(
                diagonal, rows[i : i + 1, :], 0.0
            ).astype(jnp.bfloat16)

    for p in range(PARTS):
        cols = slice(p * part, (p + 1) * part)
        for c in range(CHUNKS):
            ints_copies[p * CHUNKS + c].wait()
            for k in range(c * step, (c + 1) * step):
                half = jnp.dot(
                    left_big[near(k, 0)], ints_buf[k, :, cols], preferred_element_type=jnp.float32
                ).astype(jnp.bfloat16)
                for i in range(batch):
                    half_buf[i, k * ROWS : (k + 1) * ROWS, cols] = half[i * ROWS : (i + 1) * ROWS, :]
        for i in range(batch):
            for q in range(p * part, (p + 1) * part, TILE):
                fitted = jnp.dot(
                    right_t[...], half_buf[i, :, q : q + TILE], preferred_element_type=jnp.float32
                )
                for g in range(groups):
                    start = g // 4 * quad
                    low = fitted[start + g % 4 * 8 : start + g % 4 * 8 + 8, :]
                    start += 32 + g % 4 // 2 * 8
                    high = fitted[start : start + 8, :]
                    if g % 2 == 1:
                        high = pltpu.roll(high, 4, 0)
                    fit_buf[g, i * ROWS : (i + 1) * ROWS, q : q + TILE] = jnp.concatenate(
                        [low, high], axis=0
                    ).astype(jnp.bfloat16)

    upper = batch // 2 * ROWS
    shape = (upper, LANES)
    row = lax.broadcasted_iota(jnp.int32, shape, 0)
    col = lax.broadcasted_iota(jnp.int32, shape, 1)
    from_below = (col < upper) & (col > row)
    top_half = lax.broadcasted_iota(jnp.int32, (8, LANES), 0) < 4
    own = lax.rem(me, 2)
    size = batch * ROWS
    for first_group in range(0, groups, 2):
        both = fit_buf[first_group : first_group + 2].reshape(2 * size, aux_local)
        grams = lax.dot_general(
            both, both, (((1,), (1,)), ((), ())), preferred_element_type=jnp.float32
        )
        halves = [], []
        for g in range(2):
            gram = grams[g * size : (g + 1) * size, g * size : (g + 1) * size]
            below = pltpu.roll(gram[upper:, :], upper + 1, 1)
            packed = jnp.where(from_below, below, gram[:upper, :])
            for i in range(0, batch // 2, 2):
                first = packed[i * ROWS : (i + 1) * ROWS, :]
                second = packed[(i + 1) * ROWS : (i + 2) * ROWS, :]
                mixed = jnp.where(top_half, first[8:, :], pltpu.roll(second[8:, :], 4, 0))
                halves[i // 2].extend([first[:8, :], mixed, second[:8, :]])
        low, high = (jnp.concatenate(half, axis=0) for half in halves)
        place = places[first_group] // 2
        keep_ref[place] = jnp.where(own == 0, low, high)
        send_ref[place] = jnp.where(own == 0, high, low).astype(jnp.bfloat16)


def in_place(operand):
    return pltpu.with_memory_space_constraint(operand, pltpu.HBM)


def partial_sums(ints, blk_atoms, blk_count, occ_coeff, vir_coeff, batch_ids, places):
    groups = len(places)
    slots, block, _, aux_local = ints.shape
    batch = batch_ids.shape[0]
    virs = vir_coeff.shape[1]
    basis = occ_coeff.shape[1]
    span = basis // groups
    window_atoms = (WINDOW - 1) * span // block + 1
    depth = block * block
    group_width = virs // groups
    far = pl.BlockSpec(memory_space=pltpu.HBM)
    shape = (groups // 2, batch // 2 * group_width, LANES)
    return pl.pallas_call(
        functools.partial(partial_kernel, group_width, places),
        out_shape=(
            jax.ShapeDtypeStruct(shape, jnp.float32),
            jax.ShapeDtypeStruct(shape, jnp.bfloat16),
        ),
        in_specs=[far, pl.BlockSpec(memory_space=pltpu.SMEM)] + [far] * 4,
        out_specs=[pl.BlockSpec(memory_space=pltpu.VMEM)] * 2,
        scratch_shapes=[
            pltpu.SMEM((2, slots), jnp.int32),
            pltpu.SMEM((batch,), jnp.int32),
            pltpu.VMEM((slots, depth, aux_local), jnp.bfloat16),
            pltpu.VMEM((batch, ROWS, WINDOW * span), jnp.bfloat16),
            pltpu.VMEM((WINDOW * span, virs), jnp.bfloat16),
            pltpu.VMEM((window_atoms * batch, depth), jnp.float32),
            pltpu.VMEM((window_atoms, batch * ROWS, depth), jnp.bfloat16),
            pltpu.VMEM((slots * ROWS, virs), jnp.bfloat16),
            pltpu.VMEM((virs, slots * ROWS), jnp.bfloat16),
            pltpu.VMEM((batch, slots * ROWS, aux_local), jnp.bfloat16),
            pltpu.VMEM((groups, batch * ROWS, aux_local), jnp.bfloat16),
            pltpu.SemaphoreType.DMA((2,)),
            pltpu.SemaphoreType.DMA((PARTS, CHUNKS)),
            pltpu.SemaphoreType.DMA((batch, WINDOW)),
            pltpu.SemaphoreType.DMA((WINDOW,)),
        ],
        compiler_params=pltpu.CompilerParams(vmem_limit_bytes=40 * 1024 * 1024),
    )(
        in_place(blk_atoms.T),
        blk_count,
        in_place(batch_ids),
        in_place(ints.reshape(slots, depth, aux_local)),
        in_place(occ_coeff),
        in_place(vir_coeff),
    )


def total_kernel(group_width, batch, parts_ref, out_hbm, out_buf, out_sem):
    total = jnp.sum(parts_ref[...].astype(jnp.float32), axis=0)
    upper = batch // 2 * ROWS
    top_half = lax.broadcasted_iota(jnp.int32, (8, LANES), 0) < 4
    pieces = []
    for i in range(0, batch // 2, 2):
        first, mixed, second = (
            total[(3 * (i // 2) + s) * 8 : (3 * (i // 2) + s + 1) * 8, :] for s in range(3)
        )
        pieces += [
            first,
            jnp.where(top_half, mixed, 0.0),
            second,
            jnp.where(top_half, pltpu.roll(mixed, 4, 0), 0.0),
        ]
    above = jnp.concatenate(pieces, axis=0)
    both = jnp.concatenate([above, pltpu.roll(above, upper - 1, 1)], axis=0)
    shape = (2 * upper, 2 * upper)
    row = lax.broadcasted_iota(jnp.int32, shape, 0)
    col = lax.broadcasted_iota(jnp.int32, shape, 1)
    direct = ((row < upper) & ((col >= upper) | (col <= row))) | ((row >= upper) & (col >= row))
    whole = jnp.where(direct, both, both.T)
    copies = []
    for i in range(batch):
        for c in range(0, group_width, 8):
            rows = whole[i * ROWS + c : i * ROWS + c + 8, :]
            count = min(8, group_width - c)
            for j in range(batch):
                moved = rows if j == 0 else pltpu.roll(rows, LANES - j * ROWS, 1)
                start = (i * group_width + c) * batch + j
                out_buf[pl.ds(start, count, stride=batch), :] = moved[:count, :group_width]
        if (i + 1) % (batch // 2) == 0:
            size = batch // 2 * group_width * batch
            block = pl.ds(len(copies) * size, size)
            copies.append(
                pltpu.make_async_copy(
                    out_buf.at[block, :], out_hbm.at[block, :], out_sem.at[len(copies)]
                )
            )
            copies[-1].start()
    for copy in copies:
        copy.wait()


def total_sums(parts, batch, group_width):
    rows = batch * group_width * batch
    return pl.pallas_call(
        functools.partial(total_kernel, group_width, batch),
        out_shape=jax.ShapeDtypeStruct((rows, group_width), jnp.float32),
        in_specs=[pl.BlockSpec(memory_space=pltpu.VMEM)],
        out_specs=pl.BlockSpec(memory_space=pltpu.HBM),
        scratch_shapes=[
            pltpu.VMEM((rows + 8 * batch, group_width), jnp.float32),
            pltpu.SemaphoreType.DMA((2,)),
        ],
    )(pltpu.with_memory_space_constraint(parts, pltpu.VMEM))


def half_transform(left_rows, right_rows, block_ints, live_count):
    half_ints = jnp.einsum(
        "ikm,kmnq->kinq", left_rows, block_ints, preferred_element_type=jnp.float32
    )
    slot_ids = jnp.arange(block_ints.shape[0], dtype=jnp.int32)
    half_ints = jnp.where((slot_ids < live_count)[:, None, None, None], half_ints, 0.0).astype(
        jnp.bfloat16
    )
    return jnp.einsum("knv,kinq->ivq", right_rows, half_ints, preferred_element_type=jnp.float32)


def regrouping_device(ints, blk_atoms, blk_count, occ_coeff, vir_coeff, batch_ids):
    batch_size = batch_ids.shape[0]
    block_size = ints.shape[1]
    aux_local = ints.shape[3]
    picked = jnp.take(occ_coeff, batch_ids, axis=0)
    batch_coeff = lax.all_gather(picked, "occ", axis=1, tiled=True)
    atom_total = batch_coeff.shape[1] // block_size
    left_all = batch_coeff.reshape(batch_size, atom_total, block_size)[:, blk_atoms[:, 0], :]
    vir_local = vir_coeff.shape[1]
    right_all = vir_coeff.reshape(atom_total, block_size, vir_local)[blk_atoms[:, 1]]
    live_count = blk_count[0]
    summed = half_transform(left_all, right_all, ints, live_count)
    group_count = lax.axis_size("aux")
    vir_group = vir_local // group_count
    fitted = summed.astype(jnp.bfloat16).reshape(batch_size, group_count, vir_group, aux_local)
    regrouped = lax.all_to_all(
        lax.all_to_all(fitted, "aux", split_axis=1, concat_axis=3, tiled=True),
        "occ",
        split_axis=3,
        concat_axis=2,
        tiled=True,
    )
    group_rows = regrouped[:, 0]
    group_width = group_rows.shape[1]
    flat_rows = group_rows.reshape(batch_size * group_width, group_rows.shape[2])
    kept_rows = lax.psum_scatter(
        jnp.einsum("icq,xq->cix", group_rows, flat_rows, preferred_element_type=jnp.float32),
        "occ",
        scatter_dimension=0,
        tiled=True,
    )
    pair_ints = jnp.transpose(
        kept_rows.reshape(vir_group, batch_size, batch_size, group_width), (1, 0, 2, 3)
    )[:, None]
    return pair_ints


def on_device(ints, blk_atoms, blk_count, occ_coeff, vir_coeff, batch_ids):
    if lax.axis_size("occ") > 1:
        return regrouping_device(ints, blk_atoms, blk_count, occ_coeff, vir_coeff, batch_ids)
    batch = batch_ids.shape[0]
    groups = lax.axis_size("aux")
    group_width = vir_coeff.shape[1] // groups
    order = device_order(groups)
    places = [order.index(group) for group in range(groups)]
    keep, send = partial_sums(ints, blk_atoms, blk_count, occ_coeff, vir_coeff, batch_ids, places)
    partners = [(owner, owner ^ 1) for owner in range(groups)]
    parts = (keep + lax.ppermute(send, "aux", partners)).astype(jnp.bfloat16)
    pair_shape = parts.shape
    parts = lax.all_to_all(
        parts.reshape(groups, -1, LANES),
        "aux",
        split_axis=0,
        concat_axis=0,
        tiled=True,
        axis_index_groups=[order],
    ).reshape(pair_shape)
    total = total_sums(parts, batch, group_width)
    return total.reshape(batch, 1, group_width, batch, group_width)


def solution(mesh):
    in_specs = (
        P(None, None, None, "aux"),
        P("aux", None),
        P("aux"),
        P(None, "occ"),
        P(None, "occ"),
        P(),
    )
    out_specs = P(None, "aux", "occ", None, None)
    return jax.shard_map(
        on_device, mesh=mesh, in_specs=in_specs, out_specs=out_specs, check_vma=False
    )
```

```python
import functools

import jax
import jax.numpy as jnp
from jax import lax
from jax.experimental import pallas as pl
from jax.experimental.pallas import tpu as pltpu
from jax.sharding import PartitionSpec as P

LANES = 128
ROWS = 16
WINDOW = 3
CHUNKS = ((16, 16), (32,))
PARTS = 2
EARLY = 1
PRIO = 1
TILE = 256


def device_order(count):
    order = []
    for plane in range(count // 8):
        chips = (0, 1, 3, 2) if plane % 2 == 0 else (2, 3, 1, 0)
        order += [plane * 8 + chip * 2 + core for chip in chips for core in range(2)]
    return order if len(order) == count else list(range(count))


def partial_kernel(
    group_width,
    places,
    atoms_hbm,
    count_ref,
    ids_hbm,
    ints_hbm,
    occ_hbm,
    vir_hbm,
    keep_ref,
    send_ref,
    atoms_ref,
    ids_ref,
    ints_buf,
    occ_buf,
    vir_buf,
    left_rows,
    left_big,
    right_rows,
    right_t,
    half_buf,
    fit_buf,
    small_sem,
    ints_sem,
    occ_sem,
    vir_sem,
):
    slots, depth, aux_local = ints_buf.shape
    batch = occ_buf.shape[0]
    groups = fit_buf.shape[0]
    virs = vir_buf.shape[1]
    owners = lax.axis_size("aux")
    me = lax.axis_index("aux")
    atom_total = occ_hbm.shape[1] // ROWS
    span = occ_hbm.shape[1] // owners
    span_atoms = span // ROWS
    window_atoms = left_big.shape[0]
    part = aux_local // PARTS

    small_copies = [
        pltpu.make_async_copy(source, target, small_sem.at[s])
        for s, (source, target) in enumerate(
            ((ids_hbm, ids_ref), (atoms_hbm, atoms_ref))
        )
    ]
    for copy in small_copies:
        copy.start()
    starts = [pl.multiple_of(lax.rem(me + b, owners) * span, LANES) for b in range(WINDOW)]
    vir_copies = [
        pltpu.make_async_copy(
            vir_hbm.at[pl.ds(starts[b], span), :], vir_buf.at[pl.ds(b * span, span), :], vir_sem.at[b]
        )
        for b in range(WINDOW)
    ]
    ints_copies = []
    pieces = []
    for p, sizes in enumerate(CHUNKS):
        start = 0
        for size in sizes:
            block = (pl.ds(start, size), slice(None), pl.ds(p * part, part))
            ints_copies.append(
                pltpu.make_async_copy(
                    ints_hbm.at[block], ints_buf.at[block], ints_sem.at[len(ints_copies)]
                )
            )
            pieces.append((p, start, start + size))
            start += size
    for copy in ints_copies[:EARLY]:
        copy.start(priority=PRIO)
    for copy in vir_copies:
        copy.start()
    small_copies[0].wait()
    occ_copies = []
    for i in range(batch):
        base = pl.multiple_of(ids_ref[i] & -ROWS, ROWS)
        for b in range(WINDOW):
            occ_copies.append(
                pltpu.make_async_copy(
                    occ_hbm.at[pl.ds(base, ROWS), pl.ds(starts[b], span)],
                    occ_buf.at[i, :, pl.ds(b * span, span)],
                    occ_sem.at[i, b],
                )
            )
    for copy in occ_copies:
        copy.start()
    for copy in ints_copies[EARLY:]:
        copy.start(priority=PRIO)
    for copy in small_copies[1:]:
        copy.wait()

    def near(slot, side):
        offset = atoms_ref[side, slot] - me * span_atoms
        offset = jnp.where(offset < 0, offset + atom_total, offset)
        return jnp.minimum(offset, window_atoms - 1)

    row_bits = ROWS.bit_length() - 1
    batch_bits = batch.bit_length() - 1
    quad = 4 * group_width
    wide = (quad, virs)
    row = lax.broadcasted_iota(jnp.int32, wide, 0)
    col = lax.broadcasted_iota(jnp.int32, wide, 1)
    low = (row >> 3) * group_width + (row & 7)
    high = ((row - 32) >> 2) * group_width + 8 + (row & 3)
    target = jnp.where(row < 32, low, high) - col
    spread = jnp.concatenate(
        [jnp.where(target == -start, 1.0, 0.0).astype(jnp.bfloat16) for start in range(0, virs, quad)],
        axis=0,
    )

    shape = (WINDOW * span, depth)
    row = lax.broadcasted_iota(jnp.int32, shape, 0) & (ROWS - 1)
    col = lax.broadcasted_iota(jnp.int32, shape, 1) >> row_bits
    repeat = jnp.where(row == col, 1.0, 0.0).astype(jnp.bfloat16)

    tall = (batch, batch * ROWS)
    row = lax.broadcasted_iota(jnp.int32, tall, 0)
    col = lax.broadcasted_iota(jnp.int32, tall, 1)
    wanted = jnp.zeros(tall, jnp.int32)
    for i in range(batch):
        wanted = jnp.where(row == i, i * ROWS + (ids_ref[i] & (ROWS - 1)), wanted)
    pick = jnp.where(col == wanted, 1.0, 0.0).astype(jnp.bfloat16)

    for copy in vir_copies:
        copy.wait()
    for k in range(slots):
        rows = vir_buf[pl.ds(pl.multiple_of(near(k, 1) * ROWS, ROWS), ROWS), :]
        live = jnp.where(k < count_ref[0], 1.0, 0.0).astype(jnp.bfloat16)
        right_rows[k * ROWS : (k + 1) * ROWS, :] = rows * live
    right_t[...] = lax.dot_general(
        spread, right_rows[...], (((1,), (1,)), ((), ())), preferred_element_type=jnp.float32
    ).astype(jnp.bfloat16)

    for copy in occ_copies:
        copy.wait()
    picked = jnp.dot(
        pick, occ_buf[...].reshape(batch * ROWS, WINDOW * span), preferred_element_type=jnp.float32
    )
    picked = jnp.concatenate([picked] * window_atoms, axis=0)
    row = lax.broadcasted_iota(jnp.int32, picked.shape, 0) >> batch_bits
    col = lax.broadcasted_iota(jnp.int32, picked.shape, 1) >> row_bits
    picked = jnp.where(row == col, picked, 0.0).astype(jnp.bfloat16)
    left_rows[...] = jnp.dot(picked, repeat, preferred_element_type=jnp.float32)

    shape = (ROWS, depth)
    diagonal = lax.broadcasted_iota(jnp.int32, shape, 0) == (
        lax.broadcasted_iota(jnp.int32, shape, 1) & (ROWS - 1)
    )
    for a in range(window_atoms):
        rows = left_rows[a * batch : (a + 1) * batch, :]
        for i in range(batch):
            left_big[a, i * ROWS : (i + 1) * ROWS, :] = jnp.where(
                diagonal, rows[i : i + 1, :], 0.0
            ).astype(jnp.bfloat16)

    for p in range(PARTS):
        cols = slice(p * part, (p + 1) * part)
        for copy, (piece_part, first, last) in zip(ints_copies, pieces):
            if piece_part != p:
                continue
            copy.wait()
            for k in range(first, last):
                half = jnp.dot(
                    left_big[near(k, 0)], ints_buf[k, :, cols], preferred_element_type=jnp.float32
                ).astype(jnp.bfloat16)
                for i in range(batch):
                    half_buf[i, k * ROWS : (k + 1) * ROWS, cols] = half[i * ROWS : (i + 1) * ROWS, :]
        for i in range(batch):
            for q in range(p * part, (p + 1) * part, TILE):
                fitted = jnp.dot(
                    right_t[...], half_buf[i, :, q : q + TILE], preferred_element_type=jnp.float32
                )
                for g in range(groups):
                    start = g // 4 * quad
                    low = fitted[start + g % 4 * 8 : start + g % 4 * 8 + 8, :]
                    start += 32 + g % 4 // 2 * 8
                    high = fitted[start : start + 8, :]
                    if g % 2 == 1:
                        high = pltpu.roll(high, 4, 0)
                    fit_buf[g, i * ROWS : (i + 1) * ROWS, q : q + TILE] = jnp.concatenate(
                        [low, high], axis=0
                    ).astype(jnp.bfloat16)

    upper = batch // 2 * ROWS
    shape = (upper, LANES)
    row = lax.broadcasted_iota(jnp.int32, shape, 0)
    col = lax.broadcasted_iota(jnp.int32, shape, 1)
    from_below = (col < upper) & (col > row)
    top_half = lax.broadcasted_iota(jnp.int32, (8, LANES), 0) < 4
    own = lax.rem(me, 2)
    size = batch * ROWS
    for first_group in range(0, groups, 2):
        both = fit_buf[first_group : first_group + 2].reshape(2 * size, aux_local)
        grams = lax.dot_general(
            both, both, (((1,), (1,)), ((), ())), preferred_element_type=jnp.float32
        )
        halves = [], []
        for g in range(2):
            gram = grams[g * size : (g + 1) * size, g * size : (g + 1) * size]
            below = pltpu.roll(gram[upper:, :], upper + 1, 1)
            packed = jnp.where(from_below, below, gram[:upper, :])
            for i in range(0, batch // 2, 2):
                first = packed[i * ROWS : (i + 1) * ROWS, :]
                second = packed[(i + 1) * ROWS : (i + 2) * ROWS, :]
                mixed = jnp.where(top_half, first[8:, :], pltpu.roll(second[8:, :], 4, 0))
                halves[i // 2].extend([first[:8, :], mixed, second[:8, :]])
        low, high = (jnp.concatenate(half, axis=0) for half in halves)
        place = places[first_group] // 2
        keep_ref[place] = jnp.where(own == 0, low, high)
        send_ref[place] = jnp.where(own == 0, high, low).astype(jnp.bfloat16)


def in_place(operand):
    return pltpu.with_memory_space_constraint(operand, pltpu.HBM)


def partial_sums(ints, blk_atoms, blk_count, occ_coeff, vir_coeff, batch_ids, places):
    groups = len(places)
    slots, block, _, aux_local = ints.shape
    batch = batch_ids.shape[0]
    virs = vir_coeff.shape[1]
    basis = occ_coeff.shape[1]
    span = basis // groups
    window_atoms = (WINDOW - 1) * span // block + 1
    depth = block * block
    group_width = virs // groups
    far = pl.BlockSpec(memory_space=pltpu.HBM)
    shape = (groups // 2, batch // 2 * group_width, LANES)
    return pl.pallas_call(
        functools.partial(partial_kernel, group_width, places),
        out_shape=(
            jax.ShapeDtypeStruct(shape, jnp.float32),
            jax.ShapeDtypeStruct(shape, jnp.bfloat16),
        ),
        in_specs=[far, pl.BlockSpec(memory_space=pltpu.SMEM)] + [far] * 4,
        out_specs=[pl.BlockSpec(memory_space=pltpu.VMEM)] * 2,
        scratch_shapes=[
            pltpu.SMEM((2, slots), jnp.int32),
            pltpu.SMEM((batch,), jnp.int32),
            pltpu.VMEM((slots, depth, aux_local), jnp.bfloat16),
            pltpu.VMEM((batch, ROWS, WINDOW * span), jnp.bfloat16),
            pltpu.VMEM((WINDOW * span, virs), jnp.bfloat16),
            pltpu.VMEM((window_atoms * batch, depth), jnp.float32),
            pltpu.VMEM((window_atoms, batch * ROWS, depth), jnp.bfloat16),
            pltpu.VMEM((slots * ROWS, virs), jnp.bfloat16),
            pltpu.VMEM((virs, slots * ROWS), jnp.bfloat16),
            pltpu.VMEM((batch, slots * ROWS, aux_local), jnp.bfloat16),
            pltpu.VMEM((groups, batch * ROWS, aux_local), jnp.bfloat16),
            pltpu.SemaphoreType.DMA((2,)),
            pltpu.SemaphoreType.DMA((sum(map(len, CHUNKS)),)),
            pltpu.SemaphoreType.DMA((batch, WINDOW)),
            pltpu.SemaphoreType.DMA((WINDOW,)),
        ],
        compiler_params=pltpu.CompilerParams(vmem_limit_bytes=40 * 1024 * 1024),
    )(
        in_place(blk_atoms.T),
        blk_count,
        in_place(batch_ids),
        in_place(ints.reshape(slots, depth, aux_local)),
        in_place(occ_coeff),
        in_place(vir_coeff),
    )


def total_kernel(group_width, batch, parts_ref, out_hbm, out_buf, out_sem):
    total = jnp.sum(parts_ref[...].astype(jnp.float32), axis=0)
    upper = batch // 2 * ROWS
    top_half = lax.broadcasted_iota(jnp.int32, (8, LANES), 0) < 4
    pieces = []
    for i in range(0, batch // 2, 2):
        first, mixed, second = (
            total[(3 * (i // 2) + s) * 8 : (3 * (i // 2) + s + 1) * 8, :] for s in range(3)
        )
        pieces += [
            first,
            jnp.where(top_half, mixed, 0.0),
            second,
            jnp.where(top_half, pltpu.roll(mixed, 4, 0), 0.0),
        ]
    above = jnp.concatenate(pieces, axis=0)
    both = jnp.concatenate([above, pltpu.roll(above, upper - 1, 1)], axis=0)
    shape = (2 * upper, 2 * upper)
    row = lax.broadcasted_iota(jnp.int32, shape, 0)
    col = lax.broadcasted_iota(jnp.int32, shape, 1)
    direct = ((row < upper) & ((col >= upper) | (col <= row))) | ((row >= upper) & (col >= row))
    whole = jnp.where(direct, both, both.T)
    copies = []
    for i in range(batch):
        for c in range(0, group_width, 8):
            rows = whole[i * ROWS + c : i * ROWS + c + 8, :]
            count = min(8, group_width - c)
            for j in range(batch):
                moved = rows if j == 0 else pltpu.roll(rows, LANES - j * ROWS, 1)
                start = (i * group_width + c) * batch + j
                out_buf[pl.ds(start, count, stride=batch), :] = moved[:count, :group_width]
        if (i + 1) % (batch // 2) == 0:
            size = batch // 2 * group_width * batch
            block = pl.ds(len(copies) * size, size)
            copies.append(
                pltpu.make_async_copy(
                    out_buf.at[block, :], out_hbm.at[block, :], out_sem.at[len(copies)]
                )
            )
            copies[-1].start()
    for copy in copies:
        copy.wait()


def total_sums(parts, batch, group_width):
    rows = batch * group_width * batch
    return pl.pallas_call(
        functools.partial(total_kernel, group_width, batch),
        out_shape=jax.ShapeDtypeStruct((rows, group_width), jnp.float32),
        in_specs=[pl.BlockSpec(memory_space=pltpu.VMEM)],
        out_specs=pl.BlockSpec(memory_space=pltpu.HBM),
        scratch_shapes=[
            pltpu.VMEM((rows + 8 * batch, group_width), jnp.float32),
            pltpu.SemaphoreType.DMA((2,)),
        ],
    )(pltpu.with_memory_space_constraint(parts, pltpu.VMEM))


def half_transform(left_rows, right_rows, block_ints, live_count):
    half_ints = jnp.einsum(
        "ikm,kmnq->kinq", left_rows, block_ints, preferred_element_type=jnp.float32
    )
    slot_ids = jnp.arange(block_ints.shape[0], dtype=jnp.int32)
    half_ints = jnp.where((slot_ids < live_count)[:, None, None, None], half_ints, 0.0).astype(
        jnp.bfloat16
    )
    return jnp.einsum("knv,kinq->ivq", right_rows, half_ints, preferred_element_type=jnp.float32)


def regrouping_device(ints, blk_atoms, blk_count, occ_coeff, vir_coeff, batch_ids):
    batch_size = batch_ids.shape[0]
    block_size = ints.shape[1]
    aux_local = ints.shape[3]
    picked = jnp.take(occ_coeff, batch_ids, axis=0)
    batch_coeff = lax.all_gather(picked, "occ", axis=1, tiled=True)
    atom_total = batch_coeff.shape[1] // block_size
    left_all = batch_coeff.reshape(batch_size, atom_total, block_size)[:, blk_atoms[:, 0], :]
    vir_local = vir_coeff.shape[1]
    right_all = vir_coeff.reshape(atom_total, block_size, vir_local)[blk_atoms[:, 1]]
    live_count = blk_count[0]
    summed = half_transform(left_all, right_all, ints, live_count)
    group_count = lax.axis_size("aux")
    vir_group = vir_local // group_count
    fitted = summed.astype(jnp.bfloat16).reshape(batch_size, group_count, vir_group, aux_local)
    regrouped = lax.all_to_all(
        lax.all_to_all(fitted, "aux", split_axis=1, concat_axis=3, tiled=True),
        "occ",
        split_axis=3,
        concat_axis=2,
        tiled=True,
    )
    group_rows = regrouped[:, 0]
    group_width = group_rows.shape[1]
    flat_rows = group_rows.reshape(batch_size * group_width, group_rows.shape[2])
    kept_rows = lax.psum_scatter(
        jnp.einsum("icq,xq->cix", group_rows, flat_rows, preferred_element_type=jnp.float32),
        "occ",
        scatter_dimension=0,
        tiled=True,
    )
    pair_ints = jnp.transpose(
        kept_rows.reshape(vir_group, batch_size, batch_size, group_width), (1, 0, 2, 3)
    )[:, None]
    return pair_ints


def on_device(ints, blk_atoms, blk_count, occ_coeff, vir_coeff, batch_ids):
    if lax.axis_size("occ") > 1:
        return regrouping_device(ints, blk_atoms, blk_count, occ_coeff, vir_coeff, batch_ids)
    batch = batch_ids.shape[0]
    groups = lax.axis_size("aux")
    group_width = vir_coeff.shape[1] // groups
    order = device_order(groups)
    places = [order.index(group) for group in range(groups)]
    keep, send = partial_sums(ints, blk_atoms, blk_count, occ_coeff, vir_coeff, batch_ids, places)
    partners = [(owner, owner ^ 1) for owner in range(groups)]
    parts = (keep + lax.ppermute(send, "aux", partners)).astype(jnp.bfloat16)
    pair_shape = parts.shape
    parts = lax.all_to_all(
        parts.reshape(groups, -1, LANES),
        "aux",
        split_axis=0,
        concat_axis=0,
        tiled=True,
        axis_index_groups=[order],
    ).reshape(pair_shape)
    total = total_sums(parts, batch, group_width)
    return total.reshape(batch, 1, group_width, batch, group_width)


def solution(mesh):
    in_specs = (
        P(None, None, None, "aux"),
        P("aux", None),
        P("aux"),
        P(None, "occ"),
        P(None, "occ"),
        P(),
    )
    out_specs = P(None, "aux", "occ", None, None)
    return jax.shard_map(
        on_device, mesh=mesh, in_specs=in_specs, out_specs=out_specs, check_vma=False
    )
```

```python
import functools

import jax
import jax.numpy as jnp
from jax import lax
from jax.experimental import pallas as pl
from jax.experimental.pallas import tpu as pltpu
from jax.sharding import PartitionSpec as P

LANES = 128
ROWS = 16
WINDOW = 3
CHUNKS = ((16, 16), (32,))
PARTS = 2
EARLY = 1
PRIO = 1
TILE = 256


def device_order(count):
    order = []
    for plane in range(count // 8):
        chips = (0, 1, 3, 2) if plane % 2 == 0 else (2, 3, 1, 0)
        order += [plane * 8 + chip * 2 + core for chip in chips for core in range(2)]
    return order if len(order) == count else list(range(count))


def partial_kernel(
    group_width,
    places,
    atoms_hbm,
    count_ref,
    ids_hbm,
    ints_hbm,
    occ_hbm,
    vir_hbm,
    keep_ref,
    send_ref,
    atoms_ref,
    ids_ref,
    ints_buf,
    occ_buf,
    vir_buf,
    left_rows,
    left_big,
    right_rows,
    right_t,
    half_buf,
    fit_buf,
    small_sem,
    ints_sem,
    occ_sem,
    vir_sem,
):
    slots, depth, aux_local = ints_buf.shape
    batch = occ_buf.shape[0]
    groups = fit_buf.shape[0]
    virs = vir_buf.shape[1]
    owners = lax.axis_size("aux")
    me = lax.axis_index("aux")
    atom_total = occ_hbm.shape[1] // ROWS
    span = occ_hbm.shape[1] // owners
    span_atoms = span // ROWS
    window_atoms = left_big.shape[0]
    part = aux_local // PARTS

    small_copies = [
        pltpu.make_async_copy(source, target, small_sem.at[s])
        for s, (source, target) in enumerate(
            ((ids_hbm, ids_ref), (atoms_hbm, atoms_ref))
        )
    ]
    starts = [pl.multiple_of(lax.rem(me + b, owners) * span, LANES) for b in range(WINDOW)]
    vir_copies = [
        pltpu.make_async_copy(
            vir_hbm.at[pl.ds(starts[b], span), :], vir_buf.at[pl.ds(b * span, span), :], vir_sem.at[b]
        )
        for b in range(WINDOW)
    ]
    ints_copies = []
    pieces = []
    for p, sizes in enumerate(CHUNKS):
        start = 0
        for size in sizes:
            block = (pl.ds(start, size), slice(None), pl.ds(p * part, part))
            ints_copies.append(
                pltpu.make_async_copy(
                    ints_hbm.at[block], ints_buf.at[block], ints_sem.at[len(ints_copies)]
                )
            )
            pieces.append((p, start, start + size))
            start += size
    for copy in ints_copies[:EARLY]:
        copy.start(priority=PRIO)
    for copy in small_copies:
        copy.start()
    for copy in vir_copies:
        copy.start()
    small_copies[0].wait()
    occ_copies = []
    for i in range(batch):
        base = pl.multiple_of(ids_ref[i] & -ROWS, ROWS)
        for b in range(WINDOW):
            occ_copies.append(
                pltpu.make_async_copy(
                    occ_hbm.at[pl.ds(base, ROWS), pl.ds(starts[b], span)],
                    occ_buf.at[i, :, pl.ds(b * span, span)],
                    occ_sem.at[i, b],
                )
            )
    for copy in occ_copies:
        copy.start()
    for copy in ints_copies[EARLY:]:
        copy.start(priority=PRIO)
    for copy in small_copies[1:]:
        copy.wait()

    def near(slot, side):
        offset = atoms_ref[side, slot] - me * span_atoms
        offset = jnp.where(offset < 0, offset + atom_total, offset)
        return jnp.minimum(offset, window_atoms - 1)

    row_bits = ROWS.bit_length() - 1
    batch_bits = batch.bit_length() - 1
    quad = 4 * group_width
    wide = (quad, virs)
    row = lax.broadcasted_iota(jnp.int32, wide, 0)
    col = lax.broadcasted_iota(jnp.int32, wide, 1)
    low = (row >> 3) * group_width + (row & 7)
    high = ((row - 32) >> 2) * group_width + 8 + (row & 3)
    target = jnp.where(row < 32, low, high) - col
    spread = jnp.concatenate(
        [jnp.where(target == -start, 1.0, 0.0).astype(jnp.bfloat16) for start in range(0, virs, quad)],
        axis=0,
    )

    shape = (WINDOW * span, depth)
    row = lax.broadcasted_iota(jnp.int32, shape, 0) & (ROWS - 1)
    col = lax.broadcasted_iota(jnp.int32, shape, 1) >> row_bits
    repeat = jnp.where(row == col, 1.0, 0.0).astype(jnp.bfloat16)

    tall = (batch, batch * ROWS)
    row = lax.broadcasted_iota(jnp.int32, tall, 0)
    col = lax.broadcasted_iota(jnp.int32, tall, 1)
    wanted = jnp.zeros(tall, jnp.int32)
    for i in range(batch):
        wanted = jnp.where(row == i, i * ROWS + (ids_ref[i] & (ROWS - 1)), wanted)
    pick = jnp.where(col == wanted, 1.0, 0.0).astype(jnp.bfloat16)

    for copy in vir_copies:
        copy.wait()
    for k in range(slots):
        rows = vir_buf[pl.ds(pl.multiple_of(near(k, 1) * ROWS, ROWS), ROWS), :]
        live = jnp.where(k < count_ref[0], 1.0, 0.0).astype(jnp.bfloat16)
        right_rows[k * ROWS : (k + 1) * ROWS, :] = rows * live
    right_t[...] = lax.dot_general(
        spread, right_rows[...], (((1,), (1,)), ((), ())), preferred_element_type=jnp.float32
    ).astype(jnp.bfloat16)

    for copy in occ_copies:
        copy.wait()
    picked = jnp.dot(
        pick, occ_buf[...].reshape(batch * ROWS, WINDOW * span), preferred_element_type=jnp.float32
    )
    picked = jnp.concatenate([picked] * window_atoms, axis=0)
    row = lax.broadcasted_iota(jnp.int32, picked.shape, 0) >> batch_bits
    col = lax.broadcasted_iota(jnp.int32, picked.shape, 1) >> row_bits
    picked = jnp.where(row == col, picked, 0.0).astype(jnp.bfloat16)
    left_rows[...] = jnp.dot(picked, repeat, preferred_element_type=jnp.float32)

    shape = (ROWS, depth)
    diagonal = lax.broadcasted_iota(jnp.int32, shape, 0) == (
        lax.broadcasted_iota(jnp.int32, shape, 1) & (ROWS - 1)
    )
    for a in range(window_atoms):
        rows = left_rows[a * batch : (a + 1) * batch, :]
        for i in range(batch):
            left_big[a, i * ROWS : (i + 1) * ROWS, :] = jnp.where(
                diagonal, rows[i : i + 1, :], 0.0
            ).astype(jnp.bfloat16)

    for p in range(PARTS):
        cols = slice(p * part, (p + 1) * part)
        for copy, (piece_part, first, last) in zip(ints_copies, pieces):
            if piece_part != p:
                continue
            copy.wait()
            for k in range(first, last):
                half = jnp.dot(
                    left_big[near(k, 0)], ints_buf[k, :, cols], preferred_element_type=jnp.float32
                ).astype(jnp.bfloat16)
                for i in range(batch):
                    half_buf[i, k * ROWS : (k + 1) * ROWS, cols] = half[i * ROWS : (i + 1) * ROWS, :]
        for i in range(batch):
            for q in range(p * part, (p + 1) * part, TILE):
                fitted = jnp.dot(
                    right_t[...], half_buf[i, :, q : q + TILE], preferred_element_type=jnp.float32
                )
                for g in range(groups):
                    start = g // 4 * quad
                    low = fitted[start + g % 4 * 8 : start + g % 4 * 8 + 8, :]
                    start += 32 + g % 4 // 2 * 8
                    high = fitted[start : start + 8, :]
                    if g % 2 == 1:
                        high = pltpu.roll(high, 4, 0)
                    fit_buf[g, i * ROWS : (i + 1) * ROWS, q : q + TILE] = jnp.concatenate(
                        [low, high], axis=0
                    ).astype(jnp.bfloat16)

    upper = batch // 2 * ROWS
    shape = (upper, LANES)
    row = lax.broadcasted_iota(jnp.int32, shape, 0)
    col = lax.broadcasted_iota(jnp.int32, shape, 1)
    from_below = (col < upper) & (col > row)
    top_half = lax.broadcasted_iota(jnp.int32, (8, LANES), 0) < 4
    own = lax.rem(me, 2)
    size = batch * ROWS
    for first_group in range(0, groups, 2):
        both = fit_buf[first_group : first_group + 2].reshape(2 * size, aux_local)
        grams = lax.dot_general(
            both, both, (((1,), (1,)), ((), ())), preferred_element_type=jnp.float32
        )
        halves = [], []
        for g in range(2):
            gram = grams[g * size : (g + 1) * size, g * size : (g + 1) * size]
            below = pltpu.roll(gram[upper:, :], upper + 1, 1)
            packed = jnp.where(from_below, below, gram[:upper, :])
            for i in range(0, batch // 2, 2):
                first = packed[i * ROWS : (i + 1) * ROWS, :]
                second = packed[(i + 1) * ROWS : (i + 2) * ROWS, :]
                mixed = jnp.where(top_half, first[8:, :], pltpu.roll(second[8:, :], 4, 0))
                halves[i // 2].extend([first[:8, :], mixed, second[:8, :]])
        low, high = (jnp.concatenate(half, axis=0) for half in halves)
        place = places[first_group] // 2
        keep_ref[place] = jnp.where(own == 0, low, high)
        send_ref[place] = jnp.where(own == 0, high, low).astype(jnp.bfloat16)


def in_place(operand):
    return pltpu.with_memory_space_constraint(operand, pltpu.HBM)


def partial_sums(ints, blk_atoms, blk_count, occ_coeff, vir_coeff, batch_ids, places):
    groups = len(places)
    slots, block, _, aux_local = ints.shape
    batch = batch_ids.shape[0]
    virs = vir_coeff.shape[1]
    basis = occ_coeff.shape[1]
    span = basis // groups
    window_atoms = (WINDOW - 1) * span // block + 1
    depth = block * block
    group_width = virs // groups
    far = pl.BlockSpec(memory_space=pltpu.HBM)
    shape = (groups // 2, batch // 2 * group_width, LANES)
    return pl.pallas_call(
        functools.partial(partial_kernel, group_width, places),
        out_shape=(
            jax.ShapeDtypeStruct(shape, jnp.float32),
            jax.ShapeDtypeStruct(shape, jnp.bfloat16),
        ),
        in_specs=[far, pl.BlockSpec(memory_space=pltpu.SMEM)] + [far] * 4,
        out_specs=[pl.BlockSpec(memory_space=pltpu.VMEM)] * 2,
        scratch_shapes=[
            pltpu.SMEM((2, slots), jnp.int32),
            pltpu.SMEM((batch,), jnp.int32),
            pltpu.VMEM((slots, depth, aux_local), jnp.bfloat16),
            pltpu.VMEM((batch, ROWS, WINDOW * span), jnp.bfloat16),
            pltpu.VMEM((WINDOW * span, virs), jnp.bfloat16),
            pltpu.VMEM((window_atoms * batch, depth), jnp.float32),
            pltpu.VMEM((window_atoms, batch * ROWS, depth), jnp.bfloat16),
            pltpu.VMEM((slots * ROWS, virs), jnp.bfloat16),
            pltpu.VMEM((virs, slots * ROWS), jnp.bfloat16),
            pltpu.VMEM((batch, slots * ROWS, aux_local), jnp.bfloat16),
            pltpu.VMEM((groups, batch * ROWS, aux_local), jnp.bfloat16),
            pltpu.SemaphoreType.DMA((2,)),
            pltpu.SemaphoreType.DMA((sum(map(len, CHUNKS)),)),
            pltpu.SemaphoreType.DMA((batch, WINDOW)),
            pltpu.SemaphoreType.DMA((WINDOW,)),
        ],
        compiler_params=pltpu.CompilerParams(vmem_limit_bytes=40 * 1024 * 1024),
    )(
        in_place(blk_atoms.T),
        blk_count,
        in_place(batch_ids),
        in_place(ints.reshape(slots, depth, aux_local)),
        in_place(occ_coeff),
        in_place(vir_coeff),
    )


def total_kernel(group_width, batch, parts_ref, out_hbm, out_buf, out_sem):
    total = jnp.sum(parts_ref[...].astype(jnp.float32), axis=0)
    upper = batch // 2 * ROWS
    top_half = lax.broadcasted_iota(jnp.int32, (8, LANES), 0) < 4
    pieces = []
    for i in range(0, batch // 2, 2):
        first, mixed, second = (
            total[(3 * (i // 2) + s) * 8 : (3 * (i // 2) + s + 1) * 8, :] for s in range(3)
        )
        pieces += [
            first,
            jnp.where(top_half, mixed, 0.0),
            second,
            jnp.where(top_half, pltpu.roll(mixed, 4, 0), 0.0),
        ]
    above = jnp.concatenate(pieces, axis=0)
    both = jnp.concatenate([above, pltpu.roll(above, upper - 1, 1)], axis=0)
    shape = (2 * upper, 2 * upper)
    row = lax.broadcasted_iota(jnp.int32, shape, 0)
    col = lax.broadcasted_iota(jnp.int32, shape, 1)
    direct = ((row < upper) & ((col >= upper) | (col <= row))) | ((row >= upper) & (col >= row))
    whole = jnp.where(direct, both, both.T)
    copies = []
    for i in range(batch):
        for c in range(0, group_width, 8):
            rows = whole[i * ROWS + c : i * ROWS + c + 8, :]
            count = min(8, group_width - c)
            for j in range(batch):
                moved = rows if j == 0 else pltpu.roll(rows, LANES - j * ROWS, 1)
                start = (i * group_width + c) * batch + j
                out_buf[pl.ds(start, count, stride=batch), :] = moved[:count, :group_width]
        if (i + 1) % (batch // 2) == 0:
            size = batch // 2 * group_width * batch
            block = pl.ds(len(copies) * size, size)
            copies.append(
                pltpu.make_async_copy(
                    out_buf.at[block, :], out_hbm.at[block, :], out_sem.at[len(copies)]
                )
            )
            copies[-1].start()
    for copy in copies:
        copy.wait()


def total_sums(parts, batch, group_width):
    rows = batch * group_width * batch
    return pl.pallas_call(
        functools.partial(total_kernel, group_width, batch),
        out_shape=jax.ShapeDtypeStruct((rows, group_width), jnp.float32),
        in_specs=[pl.BlockSpec(memory_space=pltpu.VMEM)],
        out_specs=pl.BlockSpec(memory_space=pltpu.HBM),
        scratch_shapes=[
            pltpu.VMEM((rows + 8 * batch, group_width), jnp.float32),
            pltpu.SemaphoreType.DMA((2,)),
        ],
    )(pltpu.with_memory_space_constraint(parts, pltpu.VMEM))


def half_transform(left_rows, right_rows, block_ints, live_count):
    half_ints = jnp.einsum(
        "ikm,kmnq->kinq", left_rows, block_ints, preferred_element_type=jnp.float32
    )
    slot_ids = jnp.arange(block_ints.shape[0], dtype=jnp.int32)
    half_ints = jnp.where((slot_ids < live_count)[:, None, None, None], half_ints, 0.0).astype(
        jnp.bfloat16
    )
    return jnp.einsum("knv,kinq->ivq", right_rows, half_ints, preferred_element_type=jnp.float32)


def regrouping_device(ints, blk_atoms, blk_count, occ_coeff, vir_coeff, batch_ids):
    batch_size = batch_ids.shape[0]
    block_size = ints.shape[1]
    aux_local = ints.shape[3]
    picked = jnp.take(occ_coeff, batch_ids, axis=0)
    batch_coeff = lax.all_gather(picked, "occ", axis=1, tiled=True)
    atom_total = batch_coeff.shape[1] // block_size
    left_all = batch_coeff.reshape(batch_size, atom_total, block_size)[:, blk_atoms[:, 0], :]
    vir_local = vir_coeff.shape[1]
    right_all = vir_coeff.reshape(atom_total, block_size, vir_local)[blk_atoms[:, 1]]
    live_count = blk_count[0]
    summed = half_transform(left_all, right_all, ints, live_count)
    group_count = lax.axis_size("aux")
    vir_group = vir_local // group_count
    fitted = summed.astype(jnp.bfloat16).reshape(batch_size, group_count, vir_group, aux_local)
    regrouped = lax.all_to_all(
        lax.all_to_all(fitted, "aux", split_axis=1, concat_axis=3, tiled=True),
        "occ",
        split_axis=3,
        concat_axis=2,
        tiled=True,
    )
    group_rows = regrouped[:, 0]
    group_width = group_rows.shape[1]
    flat_rows = group_rows.reshape(batch_size * group_width, group_rows.shape[2])
    kept_rows = lax.psum_scatter(
        jnp.einsum("icq,xq->cix", group_rows, flat_rows, preferred_element_type=jnp.float32),
        "occ",
        scatter_dimension=0,
        tiled=True,
    )
    pair_ints = jnp.transpose(
        kept_rows.reshape(vir_group, batch_size, batch_size, group_width), (1, 0, 2, 3)
    )[:, None]
    return pair_ints


def on_device(ints, blk_atoms, blk_count, occ_coeff, vir_coeff, batch_ids):
    if lax.axis_size("occ") > 1:
        return regrouping_device(ints, blk_atoms, blk_count, occ_coeff, vir_coeff, batch_ids)
    batch = batch_ids.shape[0]
    groups = lax.axis_size("aux")
    group_width = vir_coeff.shape[1] // groups
    order = device_order(groups)
    places = [order.index(group) for group in range(groups)]
    keep, send = partial_sums(ints, blk_atoms, blk_count, occ_coeff, vir_coeff, batch_ids, places)
    partners = [(owner, owner ^ 1) for owner in range(groups)]
    parts = (keep + lax.ppermute(send, "aux", partners)).astype(jnp.bfloat16)
    pair_shape = parts.shape
    parts = lax.all_to_all(
        parts.reshape(groups, -1, LANES),
        "aux",
        split_axis=0,
        concat_axis=0,
        tiled=True,
        axis_index_groups=[order],
    ).reshape(pair_shape)
    total = total_sums(parts, batch, group_width)
    return total.reshape(batch, 1, group_width, batch, group_width)


def solution(mesh):
    in_specs = (
        P(None, None, None, "aux"),
        P("aux", None),
        P("aux"),
        P(None, "occ"),
        P(None, "occ"),
        P(),
    )
    out_specs = P(None, "aux", "occ", None, None)
    return jax.shard_map(
        on_device, mesh=mesh, in_specs=in_specs, out_specs=out_specs, check_vma=False
    )
```
